256 devices in a mesh: gx: 16 (over x_lo, z), gy: 16 (over y, x_hi, core).
Axes of the slice: x: 4 (x_hi: 2, x_lo: 2; x = x_hi * 2 + x_lo), y: 4, z: 8, core: 2. Of those that a mesh axis runs over, the one named last changes fastest.
Arguments:
- grad_out: bfloat16 [2048, 36864], P('gx', 'gy'), may hold values from -6 to 6
- inputs: bfloat16 [2048, 9216], P('gy', 'gx'), may hold values from -6 to 6
- weight: bfloat16 [9216, 36864], P('gx', 'gy'), may hold values from -0.0625 to 0.0625
Outputs:
- grad_in: bfloat16 [2048, 9216], P('gy', 'gx')
- grad_weight: float32 [9216, 36864], P('gx', 'gy')
The draws below stay inside these ranges and needn't reach their ends.
All inputs are finite; a program needn't handle non-finite values.
Results may differ from the reference program's by a relative error of at most 0.001.
Values may be sent and summed in bfloat16 or wider, within the bound.
No kernel may reach another device: no remote copies, remote signals or barrier semaphores. Data moves between devices by JAX's collectives and lax.ppermute only.
A program may use at most 64 MiB of HBM per device.

```python
import jax
import jax.numpy as jnp
from jax import lax

D = 9216
FF = 36864
ROWS = 2048


def strengthened(array, stream_key, source, target, shards_of, factor):
    def block_of(dim):
        return (jnp.arange(array.shape[dim]) // (array.shape[dim] // shards_of)).reshape((-1,) + (1,) * (array.ndim - 1 - dim))

    first = jax.random.permutation(stream_key, shards_of)[block_of(target)]
    other_side = (block_of(target) + shards_of // 2) % shards_of
    return jnp.where((block_of(source) == first) | (block_of(source) == other_side), factor * array, array)


def steps_of(own_key, dims, cuts, smallest, top_value):
    gain, own = 1.0, jax.random.fold_in(own_key, 6)
    for position, blocks in cuts:
        steps = jnp.exp(jax.random.uniform(jax.random.fold_in(own, position), (blocks,), jnp.float32, smallest / len(cuts), top_value / len(cuts)))
        gain = gain * jnp.repeat(steps, dims[position] // blocks).reshape([-1 if axis == position else 1 for axis in range(len(dims))])
    return gain


def noise(stream_key, extent, scale, reach, cuts=(), dtype=jnp.bfloat16):
    entries = jax.random.normal(stream_key, extent, jnp.float32) * scale
    if len(cuts) > 0:
        entries = steps_of(stream_key, extent, cuts, -0.22, 0.18) * entries
    return jnp.clip(entries, min=-reach, max=reach).astype(dtype)


def noise_with(stream_key, dims, scale, limit, split, heavy, dtype=jnp.bfloat16):
    result = scale * jax.random.normal(stream_key, dims, jnp.float32)
    if split:
        result = result * steps_of(stream_key, dims, split, -0.22, 0.18)
    return jnp.clip(strengthened(result, jax.random.fold_in(stream_key, 3), *heavy), -limit, limit).astype(dtype)


def setup_inputs(seed: int = 0) -> dict:
    streams_of = jax.random.split(jax.random.key(seed), 4)
    grad_out = noise_with(streams_of[0], (ROWS, FF), 1.0, 6.0, ((0, 16), (1, 16)), (1, 0, 16, 2.0))
    inputs = noise(streams_of[1], (ROWS, D), 1.0, 6.0, ((0, 16), (1, 16)))
    weight = noise(streams_of[2], (D, FF), D ** -0.5, 0.0625, ((0, 16), (1, 16)))
    return {"grad_out": grad_out, "inputs": inputs, "weight": weight}


def reference(grad_out, inputs, weight):
    grad_in = lax.dot_general(grad_out, weight, (((1,), (1,)), ((), ())), preferred_element_type=jnp.float32).astype(jnp.bfloat16)
    summed = lax.dot_general(inputs, grad_out, (((0,), (0,)), ((), ())), preferred_element_type=jnp.float32)
    grad_weight = summed * (1.0 / ROWS)
    return grad_in, grad_weight
```

```python
import functools

import jax
import jax.numpy as jnp
from jax import lax
from jax.experimental import pallas as pl
from jax.experimental.pallas import tpu as pltpu
from jax.sharding import PartitionSpec as P

XL, Z = 2, 8
Y, XH, C = 4, 2, 2
VMEM_LIMIT = 48 << 20


def gx_pairs(dxl, dz):
    return [
        (xl * Z + z, (xl + dxl) % XL * Z + (z + dz) % Z)
        for xl in range(XL)
        for z in range(Z)
    ]


def gy_pairs(dy, dxh, dc):
    return [
        (
            (y * XH + xh) * C + c,
            ((y + dy) % Y * XH + (xh + dxh) % XH) * C + (c + dc) % C,
        )
        for y in range(Y)
        for xh in range(XH)
        for c in range(C)
    ]


def up(t):
    return lax.ppermute(t, "gx", gx_pairs(0, 1))


def down(t):
    return lax.ppermute(t, "gx", gx_pairs(0, -1))


def across(t):
    return lax.ppermute(t, "gx", gx_pairs(1, 0))


def in_y(t, dy):
    return lax.ppermute(t, "gy", gy_pairs(dy, 0, 0))


def in_xh(t):
    return lax.ppermute(t, "gy", gy_pairs(0, 1, 0))


def in_core(t):
    return lax.ppermute(t, "gy", gy_pairs(0, 0, 1))


def partial_kernel(n, depth, rows, s_ref, w_ref, *refs):
    shards, (keep_ref, send_ref) = refs[:n], refs[n:]
    c = s_ref[0]
    values = jnp.concatenate([r[...] for r in shards], axis=0)
    for out_ref, half in ((send_ref, 1 - c), (keep_ref, c)):
        w = w_ref[pl.ds(pl.multiple_of(half * depth, depth), depth), :]
        part = lax.dot_general(
            w, values, (((1,), (1,)), ((), ())), preferred_element_type=jnp.float32
        )
        for k in range(n):
            out_ref[s_ref[1 + k]] = part[:, k * rows : (k + 1) * rows]


def partial_sums(scalars, weight, shards):
    n = len(shards)
    rows, cols = shards[0].shape
    width = weight.shape[0]
    depth = width // 2
    out = jax.ShapeDtypeStruct((n, depth, rows), jnp.float32)
    whole = pl.BlockSpec(memory_space=pltpu.VMEM)
    return pl.pallas_call(
        functools.partial(partial_kernel, n, depth, rows),
        out_shape=(out, out),
        in_specs=[pl.BlockSpec(memory_space=pltpu.SMEM)] + [whole] * (1 + n),
        out_specs=(whole, whole),
        compiler_params=pltpu.CompilerParams(vmem_limit_bytes=VMEM_LIMIT),
        cost_estimate=pl.CostEstimate(
            flops=2 * width * cols * rows * n,
            bytes_accessed=2 * cols * (width + n * rows) + 4 * n * width * rows,
            transcendentals=0,
        ),
        name="partial_sums",
    )(scalars, weight, *shards)


def weight_kernel(n, rows, scale, s_ref, mine_ref, other_ref, *refs):
    shards, out_ref, x_ref, g_ref = refs[:n], refs[n], refs[n + 1], refs[n + 2]
    count = mine_ref.shape[0]

    @pl.when(pl.program_id(0) == 0)
    def _():
        for k in range(n):
            at = s_ref[k]
            here = slice(k * rows, (k + 1) * rows)

            @pl.when(at < count)
            def _():
                x_ref[:, here] = mine_ref[jnp.minimum(at, count - 1)]

            @pl.when(at >= count)
            def _():
                x_ref[:, here] = other_ref[jnp.maximum(at - count, 0)]

    for k in range(n):
        g_ref[k * rows : (k + 1) * rows, :] = shards[k][...]
    out_ref[...] = (
        jnp.dot(x_ref[...], g_ref[...], preferred_element_type=jnp.float32) * scale
    )


def weight_sums(scalars, mine, other, shards, scale):
    n = len(shards)
    rows, cols = shards[0].shape
    width = mine.shape[1]
    tile = 384
    whole = pl.BlockSpec(memory_space=pltpu.VMEM)
    return pl.pallas_call(
        functools.partial(weight_kernel, n, rows, scale),
        out_shape=jax.ShapeDtypeStruct((width, cols), jnp.float32),
        grid=(cols // tile,),
        in_specs=[pl.BlockSpec(memory_space=pltpu.SMEM), whole, whole]
        + [pl.BlockSpec((rows, tile), lambda i: (0, i))] * n,
        out_specs=pl.BlockSpec((width, tile), lambda i: (0, i)),
        scratch_shapes=[
            pltpu.VMEM((width, n * rows), jnp.bfloat16),
            pltpu.VMEM((n * rows, tile), jnp.bfloat16),
        ],
        compiler_params=pltpu.CompilerParams(vmem_limit_bytes=VMEM_LIMIT),
        cost_estimate=pl.CostEstimate(
            flops=2 * width * cols * rows * n,
            bytes_accessed=2 * rows * n * (cols + width) + 4 * width * cols,
            transcendentals=0,
        ),
        name="weight_sums",
    )(scalars, mine, other, *shards)


def body(grad_out, inputs, weight):
    ix, iy = lax.axis_index("gx"), lax.axis_index("gy")
    xl, z = ix // Z, ix % Z
    y, xh, c = iy // (XH * C), iy // C % XH, iy % C
    rows = grad_out.shape[0]

    g = grad_out
    u1, d1, gx = up(g), down(g), across(g)
    u2, d2, ux1 = up(u1), down(d1), across(u1)
    u3, d3, dx2 = up(u2), down(d2), across(d2)
    u4, dx3, ux2 = up(u3), down(dx2), across(u2)
    ux3, dx4, dx1 = up(ux2), down(dx3), across(d1)

    mine = inputs.T[None]
    both = jnp.concatenate([mine, in_xh(mine)])
    column = jnp.concatenate([both, in_y(both, 1), in_y(both, -1), in_y(both, 2)])
    other = in_core(column)

    def where(shard):
        side, dz = shard
        x = xl if side == 0 else 1 - xl
        at = (z + dz) % Z
        return x * 2 + at // 4, at // 2 % 2, at % 2

    def of_inputs(shard):
        ty, txh, tc = where(shard)
        dy = (ty - y) % Y
        n = jnp.where(dy == 3, 1, jnp.where(dy == 0, 0, dy + 1))
        k = 2 * n + (txh != xh)
        return jnp.where(tc == c, k, k + column.shape[0])

    sets = [
        [((0, 0), g), ((1, 0), gx), ((0, 4), u4), ((1, 4), dx4)],
        [((0, 1), d1), ((1, 1), dx1), ((0, -3), u3), ((1, -3), ux3)],
        [((0, 2), d2), ((1, 2), dx2), ((0, -2), u2), ((1, -2), ux2)],
        [((0, 3), d3), ((1, 3), dx3), ((0, -1), u1), ((1, -1), ux1)],
    ]
    totals = {}
    for group in ((2, 3), (0, 1)):
        slots, shards = [c], []
        for place, k in enumerate(group):
            for shard, value in sets[k]:
                slots.append((where(shard)[0] - y) % Y * len(group) + place)
                shards.append(value)
        keep, send = partial_sums(jnp.stack(slots), weight, shards)
        got = in_core(send)
        m = len(group)

        def to(r):
            return keep[r * m : (r + 1) * m] + got[r * m : (r + 1) * m]

        total = to(0) + in_y(to(1), 1) + in_y(to(3), -1) + in_y(to(2), 2)
        for place, k in enumerate(group):
            totals[k] = total[place]

    order = [s for group in sets for s in group]
    grad_weight = weight_sums(
        jnp.stack([of_inputs(s) for s, _ in order]),
        column,
        other,
        [v for _, v in order],
        1.0 / (Y * XH * C * rows),
    )

    even, odd = z // 2 % 2 == xh, (z + 1) // 2 % 2 == xh

    def pick(p, a, b):
        return jnp.where(p, a, b)

    got = in_xh(
        jnp.stack(
            [pick(even, totals[2], totals[0]), pick(odd, totals[3], totals[1])]
        )
    )
    e = (pick(even, totals[0], totals[2]) + got[0]).astype(jnp.bfloat16)
    o = (pick(odd, totals[1], totals[3]) + got[1]).astype(jnp.bfloat16)
    first = z % 2 == c
    own = pick(first, e, o)
    back = in_core(pick(first, o, e))
    grad_in = jnp.concatenate([pick(c == 0, own, back), pick(c == 0, back, own)])
    return grad_in.T, grad_weight


def solution(mesh):
    return jax.shard_map(
        body,
        mesh=mesh,
        in_specs=(P("gx", "gy"), P("gy", "gx"), P("gx", "gy")),
        out_specs=(P("gy", "gx"), P("gx", "gy")),
        check_vma=False,
    )
```

```python
import functools

import jax
import jax.numpy as jnp
from jax import lax
from jax.experimental import pallas as pl
from jax.experimental.pallas import tpu as pltpu
from jax.sharding import PartitionSpec as P

XL, Z = 2, 8
Y, XH, C = 4, 2, 2
VMEM_LIMIT = 40 << 20


def gx_pairs(dxl, dz):
    return [
        (xl * Z + z, (xl + dxl) % XL * Z + (z + dz) % Z)
        for xl in range(XL)
        for z in range(Z)
    ]


def gy_pairs(dy, dxh, dc):
    return [
        (
            (y * XH + xh) * C + c,
            ((y + dy) % Y * XH + (xh + dxh) % XH) * C + (c + dc) % C,
        )
        for y in range(Y)
        for xh in range(XH)
        for c in range(C)
    ]


def up(t):
    return lax.ppermute(t, "gx", gx_pairs(0, 1))


def down(t):
    return lax.ppermute(t, "gx", gx_pairs(0, -1))


def across(t):
    return lax.ppermute(t, "gx", gx_pairs(1, 0))


def in_y(t, dy):
    return lax.ppermute(t, "gy", gy_pairs(dy, 0, 0))


def in_xh(t):
    return lax.ppermute(t, "gy", gy_pairs(0, 1, 0))


def in_core(t):
    return lax.ppermute(t, "gy", gy_pairs(0, 0, 1))


def params():
    return pltpu.CompilerParams(vmem_limit_bytes=VMEM_LIMIT)


ANYWHERE = pl.BlockSpec(memory_space=pl.ANY)
VECTOR = pl.BlockSpec(memory_space=pltpu.VMEM)
SCALAR = pl.BlockSpec(memory_space=pltpu.SMEM)


def tie(*values):
    n = len(values)
    return pl.pallas_call(
        lambda *refs: None,
        out_shape=[jax.ShapeDtypeStruct(v.shape, v.dtype) for v in values],
        in_specs=[ANYWHERE] * n,
        out_specs=[ANYWHERE] * n,
        input_output_aliases={k: k for k in range(n)},
        compiler_params=params(),
        name="tie",
    )(*values)


def partial_kernel(n, halves, s_ref, w_any, *refs):
    pieces = refs[: n * halves]
    keep_ref, send_ref, w_ref, g_ref, sem = refs[n * halves :]
    depth, rows = keep_ref.shape[1:]
    part = rows // halves
    w_copy = pltpu.make_async_copy(w_any, w_ref, sem.at[n * halves])
    w_copy.start()
    copies = []
    for k in range(n * halves):
        copy = pltpu.make_async_copy(
            pieces[k], g_ref.at[pl.ds(k * part, part), :], sem.at[k]
        )
        copy.start()
        copies.append(copy)
    w_copy.wait()
    c = s_ref[0]
    for first in range(0, n, 2):
        count = min(2, n - first)
        for k in range(first * halves, (first + count) * halves):
            copies[k].wait()
        values = g_ref[first * rows : (first + count) * rows, :]
        for out_ref, side in ((send_ref, 1 - c), (keep_ref, c)):
            w = w_ref[pl.ds(pl.multiple_of(side * depth, depth), depth), :]
            sums = lax.dot_general(
                w, values, (((1,), (1,)), ((), ())), preferred_element_type=jnp.float32
            )
            for k in range(count):
                out_ref[first + k] = sums[:, k * rows : (k + 1) * rows]


def partial_sums(core, weight, shards):
    n, halves = len(shards), len(shards[0])
    part, cols = shards[0][0].shape
    rows = part * halves
    width = weight.shape[0]
    depth = width // 2
    out = jax.ShapeDtypeStruct((n, depth, rows), jnp.float32)
    return pl.pallas_call(
        functools.partial(partial_kernel, n, halves),
        out_shape=(out, out),
        in_specs=[SCALAR] + [ANYWHERE] * (1 + n * halves),
        out_specs=(VECTOR, VECTOR),
        scratch_shapes=[
            pltpu.VMEM((width, cols), jnp.bfloat16),
            pltpu.VMEM((n * rows, cols), jnp.bfloat16),
            pltpu.SemaphoreType.DMA((n * halves + 1,)),
        ],
        compiler_params=params(),
        cost_estimate=pl.CostEstimate(
            flops=2 * width * cols * rows * n,
            bytes_accessed=2 * cols * (width + n * rows) + 4 * n * width * rows,
            transcendentals=0,
        ),
        name="partial_sums",
    )(core, weight, *[piece for shard in shards for piece in shard])


def place_kernel(counts, slots, s_ref, *refs):
    pairs, outs = refs[: 2 * len(counts)], refs[2 * len(counts) :]
    k = 0
    for group, n in enumerate(counts):
        keep_ref, got_ref = pairs[2 * group], pairs[2 * group + 1]
        for i in range(n):
            value = keep_ref[i] + got_ref[i]
            for r in range(len(outs)):

                @pl.when(s_ref[k] == r)
                def _(r=r, place=slots[k], value=value):
                    outs[r][place] = value

            k += 1


def place(to, slots, groups):
    counts = [kept.shape[0] for kept, _ in groups]
    out = jax.ShapeDtypeStruct(
        (max(slots) + 1,) + groups[0][0].shape[1:], jnp.float32
    )
    return pl.pallas_call(
        functools.partial(place_kernel, counts, slots),
        out_shape=[out] * Y,
        in_specs=[SCALAR] + [VECTOR] * (2 * len(counts)),
        out_specs=[VECTOR] * Y,
        compiler_params=params(),
        name="place",
    )(jnp.stack(to), *[a for pair in groups for a in pair])


def merge_kernel(s_ref, *refs):
    late, early, (keep_ref, send_ref) = refs[:Y], refs[Y : 2 * Y], refs[2 * Y :]

    def total(parts, k):
        return (parts[0][k] + parts[1][k]) + (parts[2][k] + parts[3][k])

    for k in range(2):
        a, b = total(late, k), total(early, k)
        here = s_ref[k] == 1
        keep_ref[k] = jnp.where(here, a, b)
        send_ref[k] = jnp.where(here, b, a)


def merge(scalars, late, early):
    out = jax.ShapeDtypeStruct(late[0].shape, jnp.float32)
    return pl.pallas_call(
        merge_kernel,
        out_shape=(out, out),
        in_specs=[SCALAR] + [VECTOR] * (2 * Y),
        out_specs=(VECTOR, VECTOR),
        compiler_params=params(),
        name="merge",
    )(scalars, *late, *early)


def finish_kernel(s_ref, keep_ref, got_ref, own_ref, back_ref):
    a, b = keep_ref[0] + got_ref[0], keep_ref[1] + got_ref[1]
    here = s_ref[0] == 1
    own_ref[...] = jnp.where(here, a, b).astype(own_ref.dtype)
    back_ref[...] = jnp.where(here, b, a).astype(back_ref.dtype)


def finish(scalars, keep, got):
    out = jax.ShapeDtypeStruct(keep.shape[1:], jnp.bfloat16)
    return pl.pallas_call(
        finish_kernel,
        out_shape=(out, out),
        in_specs=[SCALAR] + [VECTOR] * 2,
        out_specs=(VECTOR, VECTOR),
        compiler_params=params(),
        name="finish",
    )(scalars, keep, got)


def weight_kernel(n, part, scale, s_ref, mine_ref, other_ref, *refs):
    pieces, out_ref, x_ref, g_ref = refs[:-3], refs[-3], refs[-2], refs[-1]
    count, _, rows = mine_ref.shape

    @pl.when(pl.program_id(0) == 0)
    def _():
        for k in range(n):
            at = s_ref[k]
            here = slice(k * rows, (k + 1) * rows)

            @pl.when(at < count)
            def _():
                x_ref[:, here] = mine_ref[jnp.minimum(at, count - 1)]

            @pl.when(at >= count)
            def _():
                x_ref[:, here] = other_ref[jnp.maximum(at - count, 0)]

    for k, piece in enumerate(pieces):
        g_ref[k * part : (k + 1) * part, :] = piece[...]
    out_ref[...] = (
        jnp.dot(x_ref[...], g_ref[...], preferred_element_type=jnp.float32) * scale
    )


def weight_sums(scalars, mine, other, shards, scale):
    n, halves = len(shards), len(shards[0])
    part, cols = shards[0][0].shape
    rows = part * halves
    width = mine.shape[1]
    tile = 384
    return pl.pallas_call(
        functools.partial(weight_kernel, n, part, scale),
        out_shape=jax.ShapeDtypeStruct((width, cols), jnp.float32),
        grid=(cols // tile,),
        in_specs=[SCALAR, VECTOR, VECTOR]
        + [pl.BlockSpec((part, tile), lambda i: (0, i))] * (n * halves),
        out_specs=pl.BlockSpec((width, tile), lambda i: (0, i)),
        scratch_shapes=[
            pltpu.VMEM((width, n * rows), jnp.bfloat16),
            pltpu.VMEM((n * rows, tile), jnp.bfloat16),
        ],
        compiler_params=params(),
        cost_estimate=pl.CostEstimate(
            flops=2 * width * cols * rows * n,
            bytes_accessed=2 * rows * n * (cols + width) + 4 * width * cols,
            transcendentals=0,
        ),
        name="weight_sums",
    )(scalars, mine, other, *[piece for shard in shards for piece in shard])


def body(grad_out, inputs, weight):
    ix, iy = lax.axis_index("gx"), lax.axis_index("gy")
    xl, z = ix // Z, ix % Z
    y, xh, c = iy // (XH * C), iy // C % XH, iy % C
    rows = grad_out.shape[0]

    half = rows // 2
    a, b = {"g": grad_out[:half]}, {"g": grad_out[half:]}
    mine = inputs.T[None]

    def phase(k, h, *more):
        names = (("u1", "d1", "gx"), ("u2", "d2", "ux1"), ("u3", "d3", "dx2"))
        names += (("u4", "dx3", "ux2"), ("ux3", "dx4", "dx1"))
        sends = (("g", "g", "g"), ("u1", "d1", "u1"), ("u2", "d2", "d2"))
        sends += (("u3", "dx2", "u2"), ("ux2", "dx3", "d1"))
        s = [h[name] for name in sends[k]]
        got = tie(up(s[0]), down(s[1]), across(s[2]), *more)
        h.update(zip(names[k], got))
        return got[3:]

    (pair,) = phase(0, a, in_xh(mine))
    phase(0, b)
    both = jnp.concatenate([mine, pair])
    both, y1 = phase(1, a, both, in_y(both, 1))
    both, y3 = phase(1, b, both, in_y(both, -1))
    (y2,) = phase(2, a, in_y(both, 2))
    column = jnp.concatenate([both, y1, y3, y2])
    phase(2, b)
    column, other = phase(3, a, column, in_core(column))
    phase(3, b)

    def where(shard):
        side, dz = shard
        x = xl if side == 0 else 1 - xl
        at = (z + dz) % Z
        return x * 2 + at // 4, at // 2 % 2, at % 2

    def of_inputs(shard):
        ty, txh, tc = where(shard)
        dy = (ty - y) % Y
        n = jnp.where(dy == 3, 1, jnp.where(dy == 0, 0, dy + 1))
        k = 2 * n + (txh != xh)
        return jnp.where(tc == c, k, k + column.shape[0])

    at = {"g": (0, 0), "gx": (1, 0)}
    for k in range(1, 5):
        at[f"u{k}"], at[f"ux{k}"] = (0, -k), (1, -k)
        at[f"d{k}"], at[f"dx{k}"] = (0, k), (1, k)

    sets = (
        ("g", "gx", "u4", "dx4"),
        ("d1", "dx1", "u3", "ux3"),
        ("d2", "dx2", "u2", "ux2"),
        ("d3", "dx3", "u1", "ux1"),
    )
    core = jnp.stack([c])

    def partials(names):
        keep, send = partial_sums(core, weight, [(a[s], b[s]) for s in names])
        return keep, in_core(send)

    def ways(names):
        return [(where(at[s])[0] - y) % Y for s in names]

    def slots(names):
        return [next(k for k in range(4) if s in sets[k]) % 2 for s in names]

    def over_y(names, groups):
        parts = place(ways(names), slots(names), groups)
        return [parts[0], in_y(parts[1], 1), in_y(parts[3], -1), in_y(parts[2], 2)]

    first = sets[2] + sets[3]
    early = over_y(first, [partials(first)])
    middle, last = ("g", "gx", "u4", "d1", "u3"), ("dx4", "dx1", "ux3")
    there = partials(middle)
    phase(4, a)
    phase(4, b)
    late = over_y(middle + last, [there, partials(last)])

    order = sets[0] + sets[1] + sets[2] + sets[3]
    grad_weight = weight_sums(
        jnp.stack([of_inputs(at[s]) for s in order]),
        column,
        other,
        [(a[s], b[s]) for s in order],
        1.0 / (Y * XH * C * rows),
    )

    scalars = jnp.stack([z // 2 % 2 == xh, (z + 1) // 2 % 2 == xh]).astype(jnp.int32)
    keep, send = merge(scalars, late, early)
    own, back = finish(
        jnp.stack([z % 2 == c]).astype(jnp.int32), keep, in_xh(send)
    )
    back = in_core(back)
    grad_in = jnp.where(
        c == 0, jnp.concatenate([own, back]), jnp.concatenate([back, own])
    )
    return grad_in.T, grad_weight


def solution(mesh):
    return jax.shard_map(
        body,
        mesh=mesh,
        in_specs=(P("gx", "gy"), P("gy", "gx"), P("gx", "gy")),
        out_specs=(P("gy", "gx"), P("gx", "gy")),
        check_vma=False,
    )
```

```python
import functools

import jax
import jax.numpy as jnp
from jax import lax
from jax.experimental import pallas as pl
from jax.experimental.pallas import tpu as pltpu
from jax.sharding import PartitionSpec as P

XL, Z = 2, 8
Y, XH, C = 4, 2, 2
VMEM_LIMIT = 32 << 20
TIE_LIMIT = 63 << 20


def gx_pairs(dxl, dz):
    return [
        (xl * Z + z, (xl + dxl) % XL * Z + (z + dz) % Z)
        for xl in range(XL)
        for z in range(Z)
    ]


def gy_pairs(dy, dxh, dc):
    return [
        (
            (y * XH + xh) * C + c,
            ((y + dy) % Y * XH + (xh + dxh) % XH) * C + (c + dc) % C,
        )
        for y in range(Y)
        for xh in range(XH)
        for c in range(C)
    ]


def up(t):
    return lax.ppermute(t, "gx", gx_pairs(0, 1))


def down(t):
    return lax.ppermute(t, "gx", gx_pairs(0, -1))


def across(t):
    return lax.ppermute(t, "gx", gx_pairs(1, 0))


def in_y_pair(t):
    pairs = [
        ((y * XH + xh) * C + c, ((y ^ 1) * XH + xh) * C + c)
        for y in range(Y)
        for xh in range(XH)
        for c in range(C)
    ]
    return lax.ppermute(t, "gy", pairs)


def in_y(t, dy):
    return lax.ppermute(t, "gy", gy_pairs(dy, 0, 0))


def in_xh(t):
    return lax.ppermute(t, "gy", gy_pairs(0, 1, 0))


def in_core(t):
    return lax.ppermute(t, "gy", gy_pairs(0, 0, 1))


IN_HBM = pl.BlockSpec(memory_space=pltpu.HBM)
ANYWHERE = pl.BlockSpec(memory_space=pl.ANY)
VECTOR = pl.BlockSpec(memory_space=pltpu.VMEM)
SCALAR = pl.BlockSpec(memory_space=pltpu.SMEM)


def params(limit=VMEM_LIMIT):
    return pltpu.CompilerParams(vmem_limit_bytes=limit)


def tie(values, after):
    n = len(values)
    return pl.pallas_call(
        lambda *refs: None,
        out_shape=[jax.ShapeDtypeStruct(v.shape, v.dtype) for v in values],
        in_specs=[IN_HBM] * n + [ANYWHERE] * len(after),
        out_specs=[IN_HBM] * n,
        input_output_aliases={k: k for k in range(n)},
        compiler_params=params(TIE_LIMIT),
        name="tie",
    )(*values, *after)


def partial_kernel(places, s_ref, w_any, *refs):
    n = len(places)
    pieces = refs[:n]
    keep_ref, send_ref, w_ref, g_ref, sem = refs[n:]
    rows = keep_ref.shape[2]
    w_copy = pltpu.make_async_copy(w_any, w_ref, sem.at[n])
    w_copy.start()
    copies = []
    for k in range(n):
        copy = pltpu.make_async_copy(
            pieces[k], g_ref.at[pl.ds(k * rows, rows), :], sem.at[k]
        )
        copy.start()
        copies.append(copy)
    w_copy.wait()
    for first in range(0, n, 2):
        count = min(2, n - first)
        for k in range(first, first + count):
            copies[k].wait()
        sums = lax.dot_general(
            w_ref[...],
            g_ref[first * rows : (first + count) * rows, :],
            (((1,), (1,)), ((), ())),
            preferred_element_type=jnp.float32,
        )
        for k in range(count):
            group, slot = places[first + k]
            value = sums[:, k * rows : (k + 1) * rows]

            @pl.when(s_ref[0] == 1 - group)
            def _(slot=slot, value=value):
                keep_ref[slot] = value

            @pl.when(s_ref[0] == group)
            def _(slot=slot, value=value):
                send_ref[slot] = value


def partial_sums(first, weight, groups):
    places = [(g, k) for g, shards in enumerate(groups) for k in range(len(shards))]
    shards = [s for group in groups for s in group]
    n, slots = len(shards), max(len(group) for group in groups)
    rows, cols = shards[0].shape
    width = weight.shape[0]
    out = jax.ShapeDtypeStruct((slots, width, rows), jnp.float32)
    return pl.pallas_call(
        functools.partial(partial_kernel, places),
        out_shape=(out, out),
        in_specs=[SCALAR] + [IN_HBM] * (1 + n),
        out_specs=(VECTOR, VECTOR),
        scratch_shapes=[
            pltpu.VMEM((width, cols), jnp.bfloat16),
            pltpu.VMEM((n * rows, cols), jnp.bfloat16),
            pltpu.SemaphoreType.DMA((n + 1,)),
        ],
        compiler_params=params(),
        cost_estimate=pl.CostEstimate(
            flops=2 * width * cols * rows * n,
            bytes_accessed=2 * cols * (width + n * rows) + 8 * slots * width * rows,
            transcendentals=0,
        ),
        name="partial_sums",
    )(first, weight, *shards)


def place_kernel(counts, s_ref, *refs):
    pairs, outs = refs[: 2 * len(counts)], refs[2 * len(counts) :]
    k = 0
    for group, n in enumerate(counts):
        keep_ref, got_ref = pairs[2 * group], pairs[2 * group + 1]
        for i in range(n):
            for r, out_ref in enumerate(outs):

                @pl.when(s_ref[k] == r)
                def _(keep_ref=keep_ref, got_ref=got_ref, i=i, out_ref=out_ref):
                    out_ref[...] = keep_ref[i] + got_ref[i]

            k += 1


def place(ways, groups):
    counts = [kept.shape[0] for kept, _ in groups]
    out = jax.ShapeDtypeStruct(groups[0][0].shape[1:], jnp.float32)
    return pl.pallas_call(
        functools.partial(place_kernel, counts),
        out_shape=[out] * Y,
        in_specs=[SCALAR] + [VECTOR] * (2 * len(counts)),
        out_specs=[VECTOR] * Y,
        compiler_params=params(),
        name="place",
    )(ways, *[a for pair in groups for a in pair])


def merge_kernel(s_ref, *refs):
    late, early, (keep_ref, send_ref) = refs[:Y], refs[Y : 2 * Y], refs[-2:]

    def total(parts):
        return (parts[0][...] + parts[1][...]) + (parts[2][...] + parts[3][...])

    a, b = total(late), total(early)
    here = s_ref[0] == 1
    keep_ref[...] = jnp.where(here, a, b)
    send_ref[...] = jnp.where(here, b, a)


def merge(here, late, early, after):
    out = jax.ShapeDtypeStruct(late[0].shape, jnp.float32)
    return pl.pallas_call(
        merge_kernel,
        out_shape=(out, out),
        in_specs=[SCALAR] + [VECTOR] * (2 * Y) + [ANYWHERE] * len(after),
        out_specs=(VECTOR, VECTOR),
        compiler_params=params(),
        name="merge",
    )(here, *late, *early, *after)


def weight_kernel(n, tile, scale, s_ref, mine_ref, other_ref, *refs):
    pieces, (out_ref, token_ref) = refs[:n], refs[-7:-5]
    x_ref, g_ref, o_ref, in_sem, out_sem = refs[-5:]
    count, _, rows = mine_ref.shape
    copies = []
    for k in range(n):
        copy = pltpu.make_async_copy(
            pieces[k], g_ref.at[pl.ds(k * rows, rows), :], in_sem.at[k]
        )
        copy.start()
        copies.append(copy)
    token_ref[...] = jnp.zeros_like(token_ref)
    for k in range(n):
        at = s_ref[k]
        here = slice(k * rows, (k + 1) * rows)

        @pl.when(at < count)
        def _(at=at, here=here):
            x_ref[:, here] = mine_ref[jnp.minimum(at, count - 1)]

        @pl.when(at >= count)
        def _(at=at, here=here):
            x_ref[:, here] = other_ref[jnp.maximum(at - count, 0)]

    for copy in copies:
        copy.wait()
    results = []
    for t in range(g_ref.shape[1] // tile):
        columns = slice(t * tile, (t + 1) * tile)
        product = jnp.dot(
            x_ref[...], g_ref[:, columns], preferred_element_type=jnp.float32
        )
        o_ref[:, columns] = product * scale
        copy = pltpu.make_async_copy(
            o_ref.at[:, columns], out_ref.at[:, columns], out_sem.at[t]
        )
        copy.start()
        results.append(copy)
    for copy in results:
        copy.wait()


def weight_sums(scalars, mine, other, shards, scale, after):
    n = len(shards)
    rows, cols = shards[0].shape
    width = mine.shape[1]
    tile = 768
    return pl.pallas_call(
        functools.partial(weight_kernel, n, tile, scale),
        out_shape=(
            jax.ShapeDtypeStruct((width, cols), jnp.float32),
            jax.ShapeDtypeStruct((8, 128), jnp.float32),
        ),
        in_specs=[SCALAR, VECTOR, VECTOR] + [IN_HBM] * n + [ANYWHERE] * len(after),
        out_specs=(IN_HBM, VECTOR),
        scratch_shapes=[
            pltpu.VMEM((width, n * rows), jnp.bfloat16),
            pltpu.VMEM((n * rows, cols), jnp.bfloat16),
            pltpu.VMEM((width, cols), jnp.float32),
            pltpu.SemaphoreType.DMA((n,)),
            pltpu.SemaphoreType.DMA((cols // tile,)),
        ],
        compiler_params=params(),
        cost_estimate=pl.CostEstimate(
            flops=2 * width * cols * rows * n,
            bytes_accessed=2 * rows * n * (cols + width) + 4 * width * cols,
            transcendentals=0,
        ),
        name="weight_sums",
    )(scalars, mine, other, *shards, *after)


def body(grad_out, inputs, weight):
    ix, iy = lax.axis_index("gx"), lax.axis_index("gy")
    xl, z = ix // Z, ix % Z
    y, xh, c = iy // (XH * C), iy // C % XH, iy % C
    rows = grad_out.shape[0]

    at = {"g": (0, 0), "gx": (1, 0)}
    for k in range(1, 5):
        at[f"u{k}"], at[f"ux{k}"] = (0, -k), (1, -k)
        at[f"d{k}"], at[f"dx{k}"] = (0, k), (1, k)

    def where(name):
        side, dz = at[name]
        x = xl if side == 0 else 1 - xl
        place = (z + dz) % Z
        return x * 2 + place // 4, place // 2 % 2, place % 2

    sets = (
        ("g", "gx", "u4", "dx4"),
        ("d1", "dx1", "u3", "ux3"),
        ("d2", "dx2", "u2", "ux2"),
        ("d3", "dx3", "u1", "ux1"),
    )
    even = z % 2 == c
    first = jnp.stack([even]).astype(jnp.int32)
    h = {"g": grad_out}

    def partials(a, b):
        return partial_sums(first, weight, ([h[s] for s in a], [h[s] for s in b]))

    def ways(*groups):
        slots = []
        for a, b in groups:
            for k in range(max(len(a), len(b))):
                way = [(where(s[k])[0] - y) % Y if k < len(s) else -1 for s in (a, b)]
                slots.append(jnp.where(even, way[0], way[1]))
        return jnp.stack(slots).astype(jnp.int32)

    def over_y(parts):
        return [parts[0], in_y(parts[1], 1), in_y(parts[3], -1), in_y(parts[2], 2)]

    def phase(names, sends, *after):
        s = [h[name] for name in sends]
        h.update(zip(names, tie([up(s[0]), down(s[1]), across(s[2])], after)))

    mine = inputs.T[None]
    pair = in_xh(mine)
    phase(("u1", "d1", "gx"), ("g", "g", "g"), pair)
    pair = jnp.concatenate([mine, pair])
    quad = in_y_pair(pair)
    phase(("u2", "d2", "ux1"), ("u1", "d1", "u1"), quad)
    quad = jnp.concatenate([pair, quad])
    column = in_y(quad, 2)
    phase(("u3", "d3", "dx2"), ("u2", "d2", "d2"), column)
    column = jnp.concatenate([quad, column])
    other = in_core(column)

    early_a = (("d2", "dx2", "u2"), ("d3", "u1", "ux1"))
    early_b = (("ux2",), ("dx3",))
    late_a = (("g", "gx", "u4"), ("d1", "u3"))
    late_b = (("dx4",), ("dx1", "ux3"))

    keep_a, send_a = partials(*early_a)
    got_a = in_core(send_a)
    phase(("u4", "dx3", "ux2"), ("u3", "dx2", "u2"), other, keep_a, got_a)
    keep_b, send_b = partials(*early_b)
    early = place(
        ways(early_a, early_b), [(keep_a, got_a), (keep_b, in_core(send_b))]
    )
    keep_c, send_c = partials(*late_a)
    got_c = in_core(send_c)
    phase(("ux3", "dx4", "dx1"), ("ux2", "dx3", "d1"), keep_c, *early)
    early = over_y(early)
    keep_d, send_d = partials(*late_b)
    late = place(ways(late_a, late_b), [(keep_c, got_c), (keep_d, in_core(send_d))])

    def of_inputs(name):
        ty, txh, tc = where(name)
        k = (ty // 2 != y // 2) * 4 + (ty % 2 != y % 2) * 2 + (txh != xh)
        return jnp.where(tc == c, k, k + column.shape[0])

    order = [s for names in sets for s in names]
    grad_weight, token = weight_sums(
        jnp.stack([of_inputs(s) for s in order]),
        column,
        other,
        [h[s] for s in order],
        1.0 / (Y * XH * C * rows),
        late,
    )

    here = (z + jnp.where(even, 0, 1)) // 2 % 2 == xh
    keep, send = merge(
        jnp.stack([here]).astype(jnp.int32), over_y(late), early, [token]
    )
    grad_in = (keep + in_xh(send)).astype(jnp.bfloat16)
    return grad_in.T, grad_weight


def solution(mesh):
    return jax.shard_map(
        body,
        mesh=mesh,
        in_specs=(P("gx", "gy"), P("gy", "gx"), P("gx", "gy")),
        out_specs=(P("gy", "gx"), P("gx", "gy")),
        check_vma=False,
    )
```

```python
import functools

import jax
import jax.numpy as jnp
from jax import lax
from jax.experimental import pallas as pl
from jax.experimental.pallas import tpu as pltpu
from jax.sharding import PartitionSpec as P

XL, Z = 2, 8
Y, XH, C = 4, 2, 2
VMEM_LIMIT = 63 << 20


def gx_pairs(dxl, dz):
    return [
        (xl * Z + z, (xl + dxl) % XL * Z + (z + dz) % Z)
        for xl in range(XL)
        for z in range(Z)
    ]


def gy_pairs(dy, dxh, dc):
    return [
        (
            (y * XH + xh) * C + c,
            ((y + dy) % Y * XH + (xh + dxh) % XH) * C + (c + dc) % C,
        )
        for y in range(Y)
        for xh in range(XH)
        for c in range(C)
    ]


def up(t):
    return lax.ppermute(t, "gx", gx_pairs(0, 1))


def down(t):
    return lax.ppermute(t, "gx", gx_pairs(0, -1))


def across(t):
    return lax.ppermute(t, "gx", gx_pairs(1, 0))


def in_y_pair(t):
    pairs = [
        ((y * XH + xh) * C + c, ((y ^ 1) * XH + xh) * C + c)
        for y in range(Y)
        for xh in range(XH)
        for c in range(C)
    ]
    return lax.ppermute(t, "gy", pairs)


def in_y(t, dy):
    return lax.ppermute(t, "gy", gy_pairs(dy, 0, 0))


def in_xh(t):
    return lax.ppermute(t, "gy", gy_pairs(0, 1, 0))


def in_core(t):
    return lax.ppermute(t, "gy", gy_pairs(0, 0, 1))


IN_HBM = pl.BlockSpec(memory_space=pltpu.HBM)
ANYWHERE = pl.BlockSpec(memory_space=pl.ANY)
VECTOR = pl.BlockSpec(memory_space=pltpu.VMEM)
SCALAR = pl.BlockSpec(memory_space=pltpu.SMEM)


def params():
    return pltpu.CompilerParams(vmem_limit_bytes=VMEM_LIMIT)


def tie(values, after):
    n = len(values)
    return pl.pallas_call(
        lambda *refs: None,
        out_shape=[jax.ShapeDtypeStruct(v.shape, v.dtype) for v in values],
        in_specs=[IN_HBM] * n + [ANYWHERE] * len(after),
        out_specs=[IN_HBM] * n,
        input_output_aliases={k: k for k in range(n)},
        compiler_params=params(),
        name="tie",
    )(*values, *after)


def stack_kernel(a_ref, b_ref, *refs):
    out_ref, sem = refs[-2:]
    n = a_ref.shape[0]
    copies = [
        pltpu.make_async_copy(a_ref, out_ref.at[pl.ds(0, n)], sem.at[0]),
        pltpu.make_async_copy(b_ref, out_ref.at[pl.ds(n, n)], sem.at[1]),
    ]
    for copy in copies:
        copy.start()
    for copy in copies:
        copy.wait()


def stack(a, b, after):
    return pl.pallas_call(
        stack_kernel,
        out_shape=jax.ShapeDtypeStruct((2 * a.shape[0],) + a.shape[1:], a.dtype),
        in_specs=[IN_HBM] * 2 + [ANYWHERE] * len(after),
        out_specs=IN_HBM,
        scratch_shapes=[pltpu.SemaphoreType.DMA((2,))],
        compiler_params=params(),
        name="stack",
    )(a, b, *after)


def partial_kernel(places, s_ref, w_any, *refs):
    n = len(places)
    pieces = refs[:n]
    keep_ref, send_ref, w_ref, g_ref, sem = refs[-5:]
    rows = keep_ref.shape[2]
    w_copy = pltpu.make_async_copy(w_any, w_ref, sem.at[n])
    w_copy.start()
    copies = []
    for k in range(n):
        copy = pltpu.make_async_copy(
            pieces[k], g_ref.at[pl.ds(k * rows, rows), :], sem.at[k]
        )
        copy.start()
        copies.append(copy)
    w_copy.wait()
    for first in range(0, n, 2):
        count = min(2, n - first)
        for k in range(first, first + count):
            copies[k].wait()
        sums = lax.dot_general(
            w_ref[...],
            g_ref[first * rows : (first + 2) * rows, :],
            (((1,), (1,)), ((), ())),
            preferred_element_type=jnp.float32,
        )
        for k in range(count):
            group, slot = places[first + k]
            value = sums[:, k * rows : (k + 1) * rows]

            @pl.when(s_ref[0] == 1 - group)
            def _(slot=slot, value=value):
                keep_ref[slot] = value

            @pl.when(s_ref[0] == group)
            def _(slot=slot, value=value):
                send_ref[slot] = value


def partial_sums(first, weight, groups, after):
    places = [(g, k) for g, shards in enumerate(groups) for k in range(len(shards))]
    shards = [s for group in groups for s in group]
    n, slots = len(shards), max(len(group) for group in groups)
    rows, cols = shards[0].shape
    width = weight.shape[0]
    out = jax.ShapeDtypeStruct((slots, width, rows), jnp.float32)
    return pl.pallas_call(
        functools.partial(partial_kernel, places),
        out_shape=(out, out),
        in_specs=[SCALAR] + [IN_HBM] * (1 + n) + [ANYWHERE] * len(after),
        out_specs=(VECTOR, VECTOR),
        scratch_shapes=[
            pltpu.VMEM((width, cols), jnp.bfloat16),
            pltpu.VMEM(((n + n % 2) * rows, cols), jnp.bfloat16),
            pltpu.SemaphoreType.DMA((n + 1,)),
        ],
        compiler_params=params(),
        cost_estimate=pl.CostEstimate(
            flops=2 * width * cols * rows * n,
            bytes_accessed=2 * cols * (width + n * rows) + 8 * slots * width * rows,
            transcendentals=0,
        ),
        name="partial_sums",
    )(first, weight, *shards, *after)


def place_kernel(counts, s_ref, *refs):
    pairs, outs = refs[: 2 * len(counts)], refs[2 * len(counts) :]
    k = 0
    for group, n in enumerate(counts):
        keep_ref, got_ref = pairs[2 * group], pairs[2 * group + 1]
        for i in range(n):
            for r, out_ref in enumerate(outs):

                @pl.when(s_ref[k] == r)
                def _(keep_ref=keep_ref, got_ref=got_ref, i=i, out_ref=out_ref):
                    out_ref[...] = keep_ref[i] + got_ref[i]

            k += 1


def place(ways, groups):
    counts = [kept.shape[0] for kept, _ in groups]
    out = jax.ShapeDtypeStruct(groups[0][0].shape[1:], jnp.float32)
    return pl.pallas_call(
        functools.partial(place_kernel, counts),
        out_shape=[out] * Y,
        in_specs=[SCALAR] + [VECTOR] * (2 * len(counts)),
        out_specs=[VECTOR] * Y,
        compiler_params=params(),
        name="place",
    )(ways, *[a for pair in groups for a in pair])


def merge_kernel(s_ref, *refs):
    late, early, (keep_ref, send_ref) = refs[:Y], refs[Y : 2 * Y], refs[-2:]

    def total(parts):
        return (parts[0][...] + parts[1][...]) + (parts[2][...] + parts[3][...])

    a, b = total(late), total(early)
    here = s_ref[0] == 1
    keep_ref[...] = jnp.where(here, a, b)
    send_ref[...] = jnp.where(here, b, a)


def merge(here, late, early, after):
    out = jax.ShapeDtypeStruct(late[0].shape, jnp.float32)
    return pl.pallas_call(
        merge_kernel,
        out_shape=(out, out),
        in_specs=[SCALAR] + [VECTOR] * (2 * Y) + [ANYWHERE] * len(after),
        out_specs=(VECTOR, VECTOR),
        compiler_params=params(),
        name="merge",
    )(here, *late, *early, *after)


def weight_kernel(n, tile, scale, s_ref, mine_ref, other_ref, *refs):
    pieces, (out_ref, token_ref) = refs[:n], refs[-7:-5]
    x_ref, g_ref, o_ref, in_sem, out_sem = refs[-5:]
    count, _, rows = mine_ref.shape
    copies = []
    for k in range(n):
        copy = pltpu.make_async_copy(
            pieces[k], g_ref.at[pl.ds(k * rows, rows), :], in_sem.at[k]
        )
        copy.start()
        copies.append(copy)
    token_ref[...] = jnp.zeros_like(token_ref)
    for k in range(n):
        at = s_ref[k]
        here = slice(k * rows, (k + 1) * rows)

        @pl.when(at < count)
        def _(at=at, here=here):
            x_ref[:, here] = mine_ref[jnp.minimum(at, count - 1)]

        @pl.when(at >= count)
        def _(at=at, here=here):
            x_ref[:, here] = other_ref[jnp.maximum(at - count, 0)]

    for copy in copies:
        copy.wait()
    results = []
    for t in range(g_ref.shape[1] // tile):
        columns = slice(t * tile, (t + 1) * tile)
        product = jnp.dot(
            x_ref[...], g_ref[:, columns], preferred_element_type=jnp.float32
        )
        o_ref[:, columns] = product * scale
        copy = pltpu.make_async_copy(
            o_ref.at[:, columns], out_ref.at[:, columns], out_sem.at[t]
        )
        copy.start()
        results.append(copy)
    for copy in results:
        copy.wait()


def weight_sums(scalars, mine, other, shards, scale, after):
    n = len(shards)
    rows, cols = shards[0].shape
    width = mine.shape[1]
    tile = 768
    return pl.pallas_call(
        functools.partial(weight_kernel, n, tile, scale),
        out_shape=(
            jax.ShapeDtypeStruct((width, cols), jnp.float32),
            jax.ShapeDtypeStruct((8, 128), jnp.float32),
        ),
        in_specs=[SCALAR, VECTOR, VECTOR] + [IN_HBM] * n + [ANYWHERE] * len(after),
        out_specs=(IN_HBM, VECTOR),
        scratch_shapes=[
            pltpu.VMEM((width, n * rows), jnp.bfloat16),
            pltpu.VMEM((n * rows, cols), jnp.bfloat16),
            pltpu.VMEM((width, cols), jnp.float32),
            pltpu.SemaphoreType.DMA((n,)),
            pltpu.SemaphoreType.DMA((cols // tile,)),
        ],
        compiler_params=params(),
        cost_estimate=pl.CostEstimate(
            flops=2 * width * cols * rows * n,
            bytes_accessed=2 * rows * n * (cols + width) + 4 * width * cols,
            transcendentals=0,
        ),
        name="weight_sums",
    )(scalars, mine, other, *shards, *after)


def body(grad_out, inputs, weight):
    ix, iy = lax.axis_index("gx"), lax.axis_index("gy")
    xl, z = ix // Z, ix % Z
    y, xh, c = iy // (XH * C), iy // C % XH, iy % C
    rows = grad_out.shape[0]

    at = {"g": (0, 0), "gx": (1, 0)}
    for k in range(1, 5):
        at[f"u{k}"], at[f"ux{k}"] = (0, -k), (1, -k)
        at[f"d{k}"], at[f"dx{k}"] = (0, k), (1, k)

    def where(name):
        side, dz = at[name]
        x = xl if side == 0 else 1 - xl
        place = (z + dz) % Z
        return x * 2 + place // 4, place // 2 % 2, place % 2

    sets = (
        ("g", "gx", "u4", "dx4"),
        ("d1", "dx1", "u3", "ux3"),
        ("d2", "dx2", "u2", "ux2"),
        ("d3", "dx3", "u1", "ux1"),
    )
    even = z % 2 == c
    first = jnp.stack([even]).astype(jnp.int32)
    h = {"g": grad_out}

    def partials(a, b, *after):
        groups = [h[s] for s in a], [h[s] for s in b]
        return partial_sums(first, weight, groups, after)

    def ways(*groups):
        slots = []
        for a, b in groups:
            for k in range(max(len(a), len(b))):
                way = [(where(s[k])[0] - y) % Y if k < len(s) else -1 for s in (a, b)]
                slots.append(jnp.where(even, way[0], way[1]))
        return jnp.stack(slots).astype(jnp.int32)

    def over_y(parts):
        return [parts[0], in_y(parts[1], 1), in_y(parts[3], -1), in_y(parts[2], 2)]

    def phase(names, sends, *after):
        s = [h[name] for name in sends]
        h.update(zip(names, tie([up(s[0]), down(s[1]), across(s[2])], after)))

    mine = inputs.T[None]
    pair = in_xh(mine)
    phase(("u1", "d1", "gx"), ("g", "g", "g"), pair)
    pair = stack(mine, pair, [h["u1"]])
    quad = in_y_pair(pair)
    phase(("u2", "d2", "ux1"), ("u1", "d1", "u1"), pair)
    quad = stack(pair, quad, [h["u2"]])
    column = in_y(quad, 2)
    phase(("u3", "d3", "dx2"), ("u2", "d2", "d2"), quad)
    column = stack(quad, column, [h["u3"]])
    other = in_core(column)

    early_a = (("d2", "dx2", "u2"), ("d3", "u1", "ux1"))
    early_b = (("ux2",), ("dx3",))
    late_a = (("g", "gx", "u4"), ("d1", "u3"))
    late_b = (("dx4",), ("dx1", "ux3"))

    keep_a, send_a = partials(*early_a)
    got_a = in_core(send_a)
    phase(("u4", "dx3", "ux2"), ("u3", "dx2", "u2"), column, keep_a)
    keep_b, send_b = partials(*early_b)
    early = place(
        ways(early_a, early_b), [(keep_a, got_a), (keep_b, in_core(send_b))]
    )
    keep_c, send_c = partials(*late_a)
    got_c = in_core(send_c)
    early = over_y(early)
    phase(("ux3", "dx4", "dx1"), ("ux2", "dx3", "d1"), keep_c, other)
    keep_d, send_d = partials(*late_b, early[1], early[2])
    late = place(ways(late_a, late_b), [(keep_c, got_c), (keep_d, in_core(send_d))])

    def of_inputs(name):
        ty, txh, tc = where(name)
        k = (ty // 2 != y // 2) * 4 + (ty % 2 != y % 2) * 2 + (txh != xh)
        return jnp.where(tc == c, k, k + column.shape[0])

    order = [s for names in sets for s in names]
    grad_weight, token = weight_sums(
        jnp.stack([of_inputs(s) for s in order]),
        column,
        other,
        [h[s] for s in order],
        1.0 / (Y * XH * C * rows),
        late,
    )

    here = (z + jnp.where(even, 0, 1)) // 2 % 2 == xh
    keep, send = merge(
        jnp.stack([here]).astype(jnp.int32), over_y(late), early, [token]
    )
    grad_in = (keep + in_xh(send)).astype(jnp.bfloat16)
    return grad_in.T, grad_weight


def solution(mesh):
    return jax.shard_map(
        body,
        mesh=mesh,
        in_specs=(P("gx", "gy"), P("gy", "gx"), P("gx", "gy")),
        out_specs=(P("gy", "gx"), P("gx", "gy")),
        check_vma=False,
    )
```

```python
import functools

import jax
import jax.numpy as jnp
from jax import lax
from jax.experimental import pallas as pl
from jax.experimental.pallas import tpu as pltpu
from jax.sharding import PartitionSpec as P

XL, Z = 2, 8
Y, XH, C = 4, 2, 2
VMEM_LIMIT = 63 << 20


def gx_pairs(dxl, dz):
    return [
        (xl * Z + z, (xl + dxl) % XL * Z + (z + dz) % Z)
        for xl in range(XL)
        for z in range(Z)
    ]


def gy_pairs(dy, dxh, dc):
    return [
        (
            (y * XH + xh) * C + c,
            ((y + dy) % Y * XH + (xh + dxh) % XH) * C + (c + dc) % C,
        )
        for y in range(Y)
        for xh in range(XH)
        for c in range(C)
    ]


def up(t):
    return lax.ppermute(t, "gx", gx_pairs(0, 1))


def down(t):
    return lax.ppermute(t, "gx", gx_pairs(0, -1))


def across(t):
    return lax.ppermute(t, "gx", gx_pairs(1, 0))


def in_y_pair(t):
    pairs = [
        ((y * XH + xh) * C + c, ((y ^ 1) * XH + xh) * C + c)
        for y in range(Y)
        for xh in range(XH)
        for c in range(C)
    ]
    return lax.ppermute(t, "gy", pairs)


def in_y(t, dy):
    return lax.ppermute(t, "gy", gy_pairs(dy, 0, 0))


def in_xh(t):
    return lax.ppermute(t, "gy", gy_pairs(0, 1, 0))


def late_here(z, xh, c):
    return (z + (z % 2 != c)) // 2 % 2 == xh


def in_xh_where(t, late):
    pairs = []
    for xl in range(XL):
        for z in range(Z):
            for y in range(Y):
                for xh in range(XH):
                    for c in range(C):
                        if late_here(z, xh, c) == late:
                            at = ((xl * Z + z) * Y + y) * XH
                            pairs.append(
                                ((at + xh) * C + c, (at + 1 - xh) * C + c)
                            )
    return lax.ppermute(t, ("gx", "gy"), pairs)


def in_core(t):
    return lax.ppermute(t, "gy", gy_pairs(0, 0, 1))


IN_HBM = pl.BlockSpec(memory_space=pltpu.HBM)
ANYWHERE = pl.BlockSpec(memory_space=pl.ANY)
VECTOR = pl.BlockSpec(memory_space=pltpu.VMEM)
SCALAR = pl.BlockSpec(memory_space=pltpu.SMEM)


def params():
    return pltpu.CompilerParams(vmem_limit_bytes=VMEM_LIMIT)


def tie(values, after):
    n = len(values)
    return pl.pallas_call(
        lambda *refs: None,
        out_shape=[jax.ShapeDtypeStruct(v.shape, v.dtype) for v in values],
        in_specs=[IN_HBM] * n + [ANYWHERE] * len(after),
        out_specs=[IN_HBM] * n,
        input_output_aliases={k: k for k in range(n)},
        compiler_params=params(),
        name="tie",
    )(*values, *after)


def touch_kernel(a_ref, out_ref):
    out_ref[...] = a_ref[...]


def touch(a):
    return pl.pallas_call(
        touch_kernel,
        out_shape=jax.ShapeDtypeStruct(a.shape, a.dtype),
        in_specs=[VECTOR],
        out_specs=VECTOR,
        compiler_params=params(),
        name="touch",
    )(a)


def stack_kernel(a_ref, b_ref, *refs):
    n = a_ref.shape[0]
    refs[-1][:n] = a_ref[...]
    refs[-1][n:] = b_ref[...]


def stack(a, b, after):
    return pl.pallas_call(
        stack_kernel,
        out_shape=jax.ShapeDtypeStruct((2 * a.shape[0],) + a.shape[1:], a.dtype),
        in_specs=[VECTOR] * 2 + [ANYWHERE] * len(after),
        out_specs=VECTOR,
        compiler_params=params(),
        name="stack",
    )(a, b, *after)


PARTS = 4


def load_weight(w_any, w_ref, sem, first):
    part = w_ref.shape[0] // PARTS
    copies = []
    for k in range(PARTS):
        rows = pl.ds(k * part, part)
        copy = pltpu.make_async_copy(
            w_any.at[rows, :], w_ref.at[rows, :], sem.at[first + k]
        )
        copy.start()
        copies.append(copy)
    return copies


def product(w_ref, g_ref):
    return lax.dot_general(
        w_ref[...],
        g_ref[...],
        (((1,), (1,)), ((), ())),
        preferred_element_type=jnp.float32,
    )


def partial_kernel(places, s_ref, w_any, *refs):
    n = len(places)
    pieces = refs[:n]
    keep_ref, send_ref, w_ref, g_ref, sem = refs[-5:]
    rows = keep_ref.shape[2]
    copies = load_weight(w_any, w_ref, sem, n)
    for k in range(n):
        copy = pltpu.make_async_copy(
            pieces[k], g_ref.at[pl.ds(k * rows, rows), :], sem.at[k]
        )
        copy.start()
        copies.append(copy)
    for copy in copies:
        copy.wait()
    sums = product(w_ref, g_ref)
    for k in range(n):
        group, slot = places[k]
        value = sums[:, k * rows : (k + 1) * rows]

        @pl.when(s_ref[0] == 1 - group)
        def _(slot=slot, value=value):
            keep_ref[slot] = value

        @pl.when(s_ref[0] == group)
        def _(slot=slot, value=value):
            send_ref[slot] = value


def partial_sums(first, weight, groups, after):
    places = [(g, k) for g, shards in enumerate(groups) for k in range(len(shards))]
    shards = [s for group in groups for s in group]
    n, slots = len(shards), max(len(group) for group in groups)
    rows, cols = shards[0].shape
    width = weight.shape[0]
    out = jax.ShapeDtypeStruct((slots, width, rows), jnp.float32)
    return pl.pallas_call(
        functools.partial(partial_kernel, places),
        out_shape=(out, out),
        in_specs=[SCALAR] + [IN_HBM] * (1 + n) + [ANYWHERE] * len(after),
        out_specs=(VECTOR, VECTOR),
        scratch_shapes=[
            pltpu.VMEM((width, cols), jnp.bfloat16),
            pltpu.VMEM((n * rows, cols), jnp.bfloat16),
            pltpu.SemaphoreType.DMA((n + PARTS,)),
        ],
        compiler_params=params(),
        cost_estimate=pl.CostEstimate(
            flops=2 * width * cols * rows * n,
            bytes_accessed=2 * cols * (width + n * rows) + 8 * slots * width * rows,
            transcendentals=0,
        ),
        name="partial_sums",
    )(first, weight, *shards, *after)


def chosen_kernel(n, s_ref, w_any, *refs):
    out_ref, w_ref, g_ref, sem = refs[-4:]
    rows = out_ref.shape[2]
    copies = load_weight(w_any, w_ref, sem, n)
    for k in range(n):
        target = g_ref.at[pl.ds(k * rows, rows), :]
        for group in range(2):

            @pl.when(s_ref[0] == group)
            def _(source=refs[group * n + k], target=target, k=k):
                pltpu.make_async_copy(source, target, sem.at[k]).start()

        copies.append(pltpu.make_async_copy(refs[k], target, sem.at[k]))
    for copy in copies:
        copy.wait()
    sums = product(w_ref, g_ref)
    for k in range(n):
        out_ref[k] = sums[:, k * rows : (k + 1) * rows]


def chosen_sums(which, weight, groups, after):
    n = len(groups[0])
    rows, cols = groups[0][0].shape
    width = weight.shape[0]
    return pl.pallas_call(
        functools.partial(chosen_kernel, n),
        out_shape=jax.ShapeDtypeStruct((n, width, rows), jnp.float32),
        in_specs=[SCALAR] + [IN_HBM] * (1 + 2 * n) + [ANYWHERE] * len(after),
        out_specs=VECTOR,
        scratch_shapes=[
            pltpu.VMEM((width, cols), jnp.bfloat16),
            pltpu.VMEM((n * rows, cols), jnp.bfloat16),
            pltpu.SemaphoreType.DMA((n + PARTS,)),
        ],
        compiler_params=params(),
        cost_estimate=pl.CostEstimate(
            flops=2 * width * cols * rows * n,
            bytes_accessed=2 * cols * (width + n * rows) + 4 * n * width * rows,
            transcendentals=0,
        ),
        name="chosen_sums",
    )(which, weight, *groups[0], *groups[1], *after)


def place_kernel(counts, s_ref, *refs):
    pairs, outs = refs[: 2 * len(counts)], refs[2 * len(counts) :]
    k = 0
    for group, n in enumerate(counts):
        keep_ref, got_ref = pairs[2 * group], pairs[2 * group + 1]
        for i in range(n):
            for r, out_ref in enumerate(outs):

                @pl.when(s_ref[k] == r)
                def _(keep_ref=keep_ref, got_ref=got_ref, i=i, out_ref=out_ref):
                    out_ref[...] = keep_ref[i] + got_ref[i]

            k += 1


def place(ways, groups):
    counts = [kept.shape[0] for kept, _ in groups]
    out = jax.ShapeDtypeStruct(groups[0][0].shape[1:], jnp.float32)
    return pl.pallas_call(
        functools.partial(place_kernel, counts),
        out_shape=[out] * Y,
        in_specs=[SCALAR] + [VECTOR] * (2 * len(counts)),
        out_specs=[VECTOR] * Y,
        compiler_params=params(),
        name="place",
    )(ways, *[a for pair in groups for a in pair])


def merge_kernel(*refs):
    a, b, c, d = refs[:Y]
    refs[-1][...] = (a[...] + b[...]) + (c[...] + d[...])


def merge(parts, after):
    return pl.pallas_call(
        merge_kernel,
        out_shape=jax.ShapeDtypeStruct(parts[0].shape, jnp.float32),
        in_specs=[VECTOR] * Y + [ANYWHERE] * len(after),
        out_specs=VECTOR,
        compiler_params=params(),
        name="merge",
    )(*parts, *after)


def weight_kernel(n, tile, scale, s_ref, mine_ref, other_ref, *refs):
    pieces, (out_ref, token_ref) = refs[:n], refs[-7:-5]
    x_ref, g_ref, o_ref, in_sem, out_sem = refs[-5:]
    count, _, rows = mine_ref.shape
    copies = []
    for k in range(n):
        copy = pltpu.make_async_copy(
            pieces[k], g_ref.at[pl.ds(k * rows, rows), :], in_sem.at[k]
        )
        copy.start()
        copies.append(copy)
    token_ref[...] = jnp.zeros_like(token_ref)
    for k in range(n):
        at = s_ref[k]
        here = slice(k * rows, (k + 1) * rows)

        @pl.when(at < count)
        def _(at=at, here=here):
            x_ref[:, here] = mine_ref[jnp.minimum(at, count - 1)]

        @pl.when(at >= count)
        def _(at=at, here=here):
            x_ref[:, here] = other_ref[jnp.maximum(at - count, 0)]

    for copy in copies:
        copy.wait()
    results = []
    for t in range(g_ref.shape[1] // tile):
        columns = slice(t * tile, (t + 1) * tile)
        product = jnp.dot(
            x_ref[...], g_ref[:, columns], preferred_element_type=jnp.float32
        )
        o_ref[:, columns] = product * scale
        copy = pltpu.make_async_copy(
            o_ref.at[:, columns], out_ref.at[:, columns], out_sem.at[t]
        )
        copy.start()
        results.append(copy)
    for copy in results:
        copy.wait()


def weight_sums(scalars, mine, other, shards, scale, after):
    n = len(shards)
    rows, cols = shards[0].shape
    width = mine.shape[1]
    tile = 768
    return pl.pallas_call(
        functools.partial(weight_kernel, n, tile, scale),
        out_shape=(
            jax.ShapeDtypeStruct((width, cols), jnp.float32),
            jax.ShapeDtypeStruct((8, 128), jnp.float32),
        ),
        in_specs=[SCALAR, VECTOR, VECTOR] + [IN_HBM] * n + [ANYWHERE] * len(after),
        out_specs=(IN_HBM, VECTOR),
        scratch_shapes=[
            pltpu.VMEM((width, n * rows), jnp.bfloat16),
            pltpu.VMEM((n * rows, cols), jnp.bfloat16),
            pltpu.VMEM((width, cols), jnp.float32),
            pltpu.SemaphoreType.DMA((n,)),
            pltpu.SemaphoreType.DMA((cols // tile,)),
        ],
        compiler_params=params(),
        cost_estimate=pl.CostEstimate(
            flops=2 * width * cols * rows * n,
            bytes_accessed=2 * rows * n * (cols + width) + 4 * width * cols,
            transcendentals=0,
        ),
        name="weight_sums",
    )(scalars, mine, other, *shards, *after)


def body(grad_out, inputs, weight):
    ix, iy = lax.axis_index("gx"), lax.axis_index("gy")
    xl, z = ix // Z, ix % Z
    y, xh, c = iy // (XH * C), iy // C % XH, iy % C
    rows = grad_out.shape[0]

    at = {"g": (0, 0), "gx": (1, 0)}
    for k in range(1, 5):
        at[f"u{k}"], at[f"ux{k}"] = (0, -k), (1, -k)
        at[f"d{k}"], at[f"dx{k}"] = (0, k), (1, k)

    def where(name):
        side, dz = at[name]
        x = xl if side == 0 else 1 - xl
        place = (z + dz) % Z
        return x * 2 + place // 4, place // 2 % 2, place % 2

    sets = (
        ("g", "gx", "u4", "dx4"),
        ("d1", "dx1", "u3", "ux3"),
        ("d2", "dx2", "u2", "ux2"),
        ("d3", "dx3", "u1", "ux1"),
    )
    even = z % 2 == c
    first = jnp.stack([even]).astype(jnp.int32)
    h = {"g": grad_out}

    def partials(a, b, *after):
        groups = [h[s] for s in a], [h[s] for s in b]
        return partial_sums(first, weight, groups, after)

    def ways(*groups):
        slots = []
        for a, b in groups:
            for k in range(max(len(a), len(b), 1)):
                way = [(where(s[k])[0] - y) % Y if k < len(s) else -1 for s in (a, b)]
                slots.append(jnp.where(even, way[0], way[1]))
        return jnp.stack(slots).astype(jnp.int32)

    def over_y(parts):
        return [parts[0], in_y(parts[1], 1), in_y(parts[3], -1), in_y(parts[2], 2)]

    def phase(names, sends, *after):
        s = [h[name] for name in sends]
        h.update(zip(names, tie([up(s[0]), down(s[1]), across(s[2])], after)))

    mine = touch(inputs.T[None])
    pair = in_xh(mine)
    phase(("u1", "d1", "gx"), ("g", "g", "g"), pair)
    pair = stack(mine, pair, [h["u1"]])
    quad = in_y_pair(pair)
    phase(("u2", "d2", "ux1"), ("u1", "d1", "u1"), pair)
    quad = stack(pair, quad, [h["u2"]])
    column = in_y(quad, 2)
    first_early = (("d2", "u2"), ("u1", "ux1"))
    keep_a, send_a = partials(*first_early)
    got_a = in_core(send_a)
    phase(("u3", "d3", "dx2"), ("u2", "d2", "d2"), quad, keep_a)
    column = stack(quad, column, [h["u3"]])
    other = in_core(column)
    mixed = (("dx2", "g", "gx"), ("d3", "d1", "u3"))
    keep_b, send_b = partials(*mixed)
    got_b = in_core(send_b)
    phase(("u4", "dx3", "ux2"), ("u3", "dx2", "u2"), column, got_a, keep_b)
    last_early = (("ux2",), ("dx3",))
    keep_c, send_c = partials(*last_early)
    got_c = in_core(send_c)
    none = ((), ())
    early = place(
        ways(first_early, (mixed[0][:1], mixed[1][:1]), none, none, last_early),
        [(keep_a, got_a), (keep_b, got_b), (keep_c, got_c)],
    )
    phase(("ux3", "dx4", "dx1"), ("ux2", "dx3", "d1"), other, *early)
    early = over_y(early)
    last = (("u4", "dx4"), ("dx1", "ux3"))
    groups = [[h[s] for s in group] for group in last]
    got_d = in_core(chosen_sums(first, weight, groups, early[1:3]))
    keep_d = chosen_sums(1 - first, weight, groups, [])
    late = place(
        ways(none, (mixed[0][1:], mixed[1][1:]), last),
        [(keep_b, got_b), (keep_d, got_d)],
    )

    def of_inputs(name):
        ty, txh, tc = where(name)
        k = (ty // 2 != y // 2) * 4 + (ty % 2 != y % 2) * 2 + (txh != xh)
        return jnp.where(tc == c, k, k + column.shape[0])

    order = [s for names in sets for s in names]
    grad_weight, token = weight_sums(
        jnp.stack([of_inputs(s) for s in order]),
        column,
        other,
        [h[s] for s in order],
        1.0 / (Y * XH * C * rows),
        late,
    )

    early = merge(early, late)
    got_early = in_xh_where(early, True)
    late = merge(over_y(late), [token, got_early])
    got_late = in_xh_where(late, False)
    grad_in = jnp.where(late_here(z, xh, c), late + got_late, early + got_early)
    return grad_in.astype(jnp.bfloat16).T, grad_weight


def solution(mesh):
    return jax.shard_map(
        body,
        mesh=mesh,
        in_specs=(P("gx", "gy"), P("gy", "gx"), P("gx", "gy")),
        out_specs=(P("gy", "gx"), P("gx", "gy")),
        check_vma=False,
    )
```

```python
import functools

import jax
import jax.numpy as jnp
from jax import lax
from jax.experimental import pallas as pl
from jax.experimental.pallas import tpu as pltpu
from jax.sharding import PartitionSpec as P

XL, Z = 2, 8
Y, XH, C = 4, 2, 2
VMEM_LIMIT = 63 << 20
TAIL_LIMIT = 32 << 20
NO_COST = pl.CostEstimate(flops=1, bytes_accessed=1, transcendentals=0)


def gx_pairs(dxl, dz):
    return [
        (xl * Z + z, (xl + dxl) % XL * Z + (z + dz) % Z)
        for xl in range(XL)
        for z in range(Z)
    ]


def gy_pairs(dy, dxh, dc):
    return [
        (
            (y * XH + xh) * C + c,
            ((y + dy) % Y * XH + (xh + dxh) % XH) * C + (c + dc) % C,
        )
        for y in range(Y)
        for xh in range(XH)
        for c in range(C)
    ]


def up(t):
    return lax.ppermute(t, "gx", gx_pairs(0, 1))


def down(t):
    return lax.ppermute(t, "gx", gx_pairs(0, -1))


def across(t):
    return lax.ppermute(t, "gx", gx_pairs(1, 0))


def in_y_pair(t):
    pairs = [
        ((y * XH + xh) * C + c, ((y ^ 1) * XH + xh) * C + c)
        for y in range(Y)
        for xh in range(XH)
        for c in range(C)
    ]
    return lax.ppermute(t, "gy", pairs)


def in_y(t, dy):
    return lax.ppermute(t, "gy", gy_pairs(dy, 0, 0))


def in_xh(t):
    return lax.ppermute(t, "gy", gy_pairs(0, 1, 0))


def late_here(z, xh, c):
    return (z + (z % 2 != c)) // 2 % 2 == xh


def in_core(t):
    return lax.ppermute(t, "gy", gy_pairs(0, 0, 1))


IN_HBM = pl.BlockSpec(memory_space=pltpu.HBM)
ANYWHERE = pl.BlockSpec(memory_space=pl.ANY)
VECTOR = pl.BlockSpec(memory_space=pltpu.VMEM)
SCALAR = pl.BlockSpec(memory_space=pltpu.SMEM)


def params(limit=VMEM_LIMIT):
    return pltpu.CompilerParams(vmem_limit_bytes=limit)


def tie_kernel(*refs):
    refs[-1][...] = jnp.zeros_like(refs[-1])


def tie(values, after):
    n = len(values)
    return pl.pallas_call(
        tie_kernel,
        out_shape=[jax.ShapeDtypeStruct(v.shape, v.dtype) for v in values]
        + [jax.ShapeDtypeStruct((8, 128), jnp.float32)],
        in_specs=[IN_HBM] * n + [ANYWHERE] * len(after),
        out_specs=[IN_HBM] * n + [VECTOR],
        input_output_aliases={k: k for k in range(n)},
        compiler_params=params(),
        cost_estimate=NO_COST,
        name="tie",
    )(*values, *after)


def touch_kernel(a_ref, out_ref):
    out_ref[...] = a_ref[...]


def touch(a):
    return pl.pallas_call(
        touch_kernel,
        out_shape=jax.ShapeDtypeStruct(a.shape, a.dtype),
        in_specs=[VECTOR],
        out_specs=VECTOR,
        compiler_params=params(),
        cost_estimate=NO_COST,
        name="touch",
    )(a)


def stack_kernel(a_ref, b_ref, *refs):
    n = a_ref.shape[0]
    refs[-1][:n] = a_ref[...]
    refs[-1][n:] = b_ref[...]


def stack(a, b, after):
    return pl.pallas_call(
        stack_kernel,
        out_shape=jax.ShapeDtypeStruct((2 * a.shape[0],) + a.shape[1:], a.dtype),
        in_specs=[VECTOR] * 2 + [ANYWHERE] * len(after),
        out_specs=VECTOR,
        compiler_params=params(),
        cost_estimate=NO_COST,
        name="stack",
    )(a, b, *after)


PARTS = 4


def load_weight(w_any, w_ref, sem, first):
    part = w_ref.shape[0] // PARTS
    copies = []
    for k in range(PARTS):
        rows = pl.ds(k * part, part)
        copy = pltpu.make_async_copy(
            w_any.at[rows, :], w_ref.at[rows, :], sem.at[first + k]
        )
        copy.start()
        copies.append(copy)
    return copies


def product(w_ref, g_ref):
    return lax.dot_general(
        w_ref[...],
        g_ref[...],
        (((1,), (1,)), ((), ())),
        preferred_element_type=jnp.float32,
    )


def partial_kernel(places, s_ref, w_any, *refs):
    n = len(places)
    pieces = refs[:n]
    keep_ref, send_ref, w_ref, g_ref, sem = refs[-5:]
    rows = keep_ref.shape[2]
    copies = load_weight(w_any, w_ref, sem, n)
    for k in range(n):
        copy = pltpu.make_async_copy(
            pieces[k], g_ref.at[pl.ds(k * rows, rows), :], sem.at[k]
        )
        copy.start()
        copies.append(copy)
    for copy in copies:
        copy.wait()
    sums = product(w_ref, g_ref)
    for k in range(n):
        group, slot = places[k]
        value = sums[:, k * rows : (k + 1) * rows]

        @pl.when(s_ref[0] == 1 - group)
        def _(slot=slot, value=value):
            keep_ref[slot] = value

        @pl.when(s_ref[0] == group)
        def _(slot=slot, value=value):
            send_ref[slot] = value


def partial_sums(first, weight, groups, after):
    places = [(g, k) for g, shards in enumerate(groups) for k in range(len(shards))]
    shards = [s for group in groups for s in group]
    n, slots = len(shards), max(len(group) for group in groups)
    rows, cols = shards[0].shape
    width = weight.shape[0]
    out = jax.ShapeDtypeStruct((slots, width, rows), jnp.float32)
    return pl.pallas_call(
        functools.partial(partial_kernel, places),
        out_shape=(out, out),
        in_specs=[SCALAR] + [IN_HBM] * (1 + n) + [ANYWHERE] * len(after),
        out_specs=(VECTOR, VECTOR),
        scratch_shapes=[
            pltpu.VMEM((width, cols), jnp.bfloat16),
            pltpu.VMEM((n * rows, cols), jnp.bfloat16),
            pltpu.SemaphoreType.DMA((n + PARTS,)),
        ],
        compiler_params=params(),
        cost_estimate=NO_COST,
        name="partial_sums",
    )(first, weight, *shards, *after)


def chosen_kernel(n, own, s_ref, w_any, *refs):
    out_ref, w_ref, g_ref, sem = refs[-4:]
    rows = out_ref.shape[2]
    copies = load_weight(w_any, w_ref, sem, n)
    for k in range(n):
        target = g_ref.at[pl.ds(k * rows, rows), :]
        for group in range(2):

            @pl.when((s_ref[0] == 1 - group) == own)
            def _(source=refs[group * n + k], target=target, k=k):
                pltpu.make_async_copy(source, target, sem.at[k]).start()

        copies.append(pltpu.make_async_copy(refs[k], target, sem.at[k]))
    for copy in copies:
        copy.wait()
    sums = product(w_ref, g_ref)
    for k in range(n):
        out_ref[k] = sums[:, k * rows : (k + 1) * rows]


def chosen_sums(own, scalars, weight, groups, after):
    n = len(groups[0])
    rows, cols = groups[0][0].shape
    width = weight.shape[0]
    return pl.pallas_call(
        functools.partial(chosen_kernel, n, own),
        out_shape=jax.ShapeDtypeStruct((n, width, rows), jnp.float32),
        in_specs=[SCALAR] + [IN_HBM] * (1 + 2 * n) + [ANYWHERE] * len(after),
        out_specs=VECTOR,
        scratch_shapes=[
            pltpu.VMEM((width, cols), jnp.bfloat16),
            pltpu.VMEM((n * rows, cols), jnp.bfloat16),
            pltpu.SemaphoreType.DMA((n + PARTS,)),
        ],
        compiler_params=params(),
        cost_estimate=NO_COST,
        name="chosen_sums",
    )(scalars, weight, *groups[0], *groups[1], *after)


def place_kernel(base, counts, s_ref, *refs):
    pairs, outs = refs[: 2 * len(counts)], refs[-Y:]
    k = base
    for group, n in enumerate(counts):
        keep_ref, got_ref = pairs[2 * group], pairs[2 * group + 1]
        for i in range(n):
            for r, out_ref in enumerate(outs):

                @pl.when(s_ref[k] == r)
                def _(keep_ref=keep_ref, got_ref=got_ref, i=i, out_ref=out_ref):
                    out_ref[...] = keep_ref[i] + got_ref[i]

            k += 1


def place(base, scalars, groups, limit, after):
    counts = [kept.shape[0] for kept, _ in groups]
    out = jax.ShapeDtypeStruct(groups[0][0].shape[1:], jnp.float32)
    return pl.pallas_call(
        functools.partial(place_kernel, base, counts),
        out_shape=[out] * Y,
        in_specs=[SCALAR] + [VECTOR] * (2 * len(counts)) + [ANYWHERE] * len(after),
        out_specs=[VECTOR] * Y,
        compiler_params=params(limit),
        cost_estimate=NO_COST,
        name="place",
    )(scalars, *[a for pair in groups for a in pair], *after)


def merge_kernel(base, s_ref, *refs):
    late, early, (keep_ref, send_ref) = refs[:Y], refs[Y : 2 * Y], refs[-2:]

    def total(parts):
        return (parts[0][...] + parts[1][...]) + (parts[2][...] + parts[3][...])

    a, b = total(late), total(early)
    here = s_ref[base] == 1
    keep_ref[...] = jnp.where(here, a, b)
    send_ref[...] = jnp.where(here, b, a)


def merge(base, scalars, late, early, after):
    out = jax.ShapeDtypeStruct(late[0].shape, jnp.float32)
    return pl.pallas_call(
        functools.partial(merge_kernel, base),
        out_shape=(out, out),
        in_specs=[SCALAR] + [VECTOR] * (2 * Y) + [ANYWHERE] * len(after),
        out_specs=(VECTOR, VECTOR),
        compiler_params=params(TAIL_LIMIT),
        cost_estimate=NO_COST,
        name="merge",
    )(scalars, *late, *early, *after)


def weight_kernel(base, n, tile, scale, s_ref, mine_ref, other_ref, *refs):
    pieces, (out_ref, token_ref) = refs[:n], refs[-7:-5]
    x_ref, g_ref, o_ref, in_sem, out_sem = refs[-5:]
    count, _, rows = mine_ref.shape
    copies = []
    for k in range(n):
        copy = pltpu.make_async_copy(
            pieces[k], g_ref.at[pl.ds(k * rows, rows), :], in_sem.at[k]
        )
        copy.start()
        copies.append(copy)
    token_ref[...] = jnp.zeros_like(token_ref)
    for k in range(n):
        at = s_ref[base + k]
        here = slice(k * rows, (k + 1) * rows)

        @pl.when(at < count)
        def _(at=at, here=here):
            x_ref[:, here] = mine_ref[jnp.minimum(at, count - 1)]

        @pl.when(at >= count)
        def _(at=at, here=here):
            x_ref[:, here] = other_ref[jnp.maximum(at - count, 0)]

    for copy in copies:
        copy.wait()
    results = []
    for t in range(g_ref.shape[1] // tile):
        columns = slice(t * tile, (t + 1) * tile)
        product = jnp.dot(
            x_ref[...], g_ref[:, columns], preferred_element_type=jnp.float32
        )
        o_ref[:, columns] = product * scale
        copy = pltpu.make_async_copy(
            o_ref.at[:, columns], out_ref.at[:, columns], out_sem.at[t]
        )
        copy.start()
        results.append(copy)
    for copy in results:
        copy.wait()


def weight_sums(base, scalars, mine, other, shards, scale, after):
    n = len(shards)
    rows, cols = shards[0].shape
    width = mine.shape[1]
    tile = 768
    return pl.pallas_call(
        functools.partial(weight_kernel, base, n, tile, scale),
        out_shape=(
            jax.ShapeDtypeStruct((width, cols), jnp.float32),
            jax.ShapeDtypeStruct((8, 128), jnp.float32),
        ),
        in_specs=[SCALAR, VECTOR, VECTOR] + [IN_HBM] * n + [ANYWHERE] * len(after),
        out_specs=(IN_HBM, VECTOR),
        scratch_shapes=[
            pltpu.VMEM((width, n * rows), jnp.bfloat16),
            pltpu.VMEM((n * rows, cols), jnp.bfloat16),
            pltpu.VMEM((width, cols), jnp.float32),
            pltpu.SemaphoreType.DMA((n,)),
            pltpu.SemaphoreType.DMA((cols // tile,)),
        ],
        compiler_params=params(TAIL_LIMIT),
        cost_estimate=NO_COST,
        name="weight_sums",
    )(scalars, mine, other, *shards, *after)


def body(grad_out, inputs, weight):
    ix, iy = lax.axis_index("gx"), lax.axis_index("gy")
    xl, z = ix // Z, ix % Z
    y, xh, c = iy // (XH * C), iy // C % XH, iy % C
    rows = grad_out.shape[0]

    at = {"g": (0, 0), "gx": (1, 0)}
    for k in range(1, 5):
        at[f"u{k}"], at[f"ux{k}"] = (0, -k), (1, -k)
        at[f"d{k}"], at[f"dx{k}"] = (0, k), (1, k)

    def where(name):
        side, dz = at[name]
        x = xl if side == 0 else 1 - xl
        place = (z + dz) % Z
        return x * 2 + place // 4, place // 2 % 2, place % 2

    sets = (
        ("g", "gx", "u4", "dx4"),
        ("d1", "dx1", "u3", "ux3"),
        ("d2", "dx2", "u2", "ux2"),
        ("d3", "dx3", "u1", "ux1"),
    )
    even = z % 2 == c
    h = {"g": grad_out}

    first_early = (("d2", "u2"), ("u1", "ux1"))
    mixed = (("dx2", "g", "gx"), ("d3", "d1", "u3"))
    last_early = (("ux2",), ("dx3",))
    last = (("u4", "dx4"), ("dx1", "ux3"))
    order = [s for names in sets for s in names]

    def ways(*groups):
        slots = []
        for a, b in groups:
            for k in range(max(len(a), len(b), 1)):
                way = [(where(s[k])[0] - y) % Y if k < len(s) else -1 for s in (a, b)]
                slots.append(jnp.where(even, way[0], way[1]))
        return slots

    def of_inputs(name):
        ty, txh, tc = where(name)
        k = (ty // 2 != y // 2) * 4 + (ty % 2 != y % 2) * 2 + (txh != xh)
        return jnp.where(tc == c, k, k + Y * XH)

    none = ((), ())
    lists = [
        [even],
        ways(first_early, (mixed[0][:1], mixed[1][:1]), none, none, last_early),
        ways(none, (mixed[0][1:], mixed[1][1:]), last),
        [of_inputs(s) for s in order],
        [late_here(z, xh, c)],
    ]
    scalars = jnp.stack([jnp.int32(v) for values in lists for v in values])
    _, at_early, at_late, at_inputs, at_here = (
        sum(len(values) for values in lists[:k]) for k in range(len(lists))
    )

    def partials(a, b, *after):
        groups = [h[s] for s in a], [h[s] for s in b]
        return partial_sums(scalars, weight, groups, after)

    def over_y(parts):
        return [parts[0], in_y(parts[1], 1), in_y(parts[3], -1), in_y(parts[2], 2)]

    def phase(names, sends, *after):
        s = [h[name] for name in sends]
        *got, token = tie([up(s[0]), down(s[1]), across(s[2])], after)
        h.update(zip(names, got))
        return token

    mine = touch(inputs.T[None])
    pair = in_xh(mine)
    phase(("u1", "d1", "gx"), ("g", "g", "g"), pair)
    pair = stack(mine, pair, [h["u1"]])
    quad = in_y_pair(pair)
    phase(("u2", "d2", "ux1"), ("u1", "d1", "u1"), pair)
    quad = stack(pair, quad, [h["u2"]])
    column = in_y(quad, 2)
    keep_a, send_a = partials(*first_early)
    got_a = in_core(send_a)
    phase(("u3", "d3", "dx2"), ("u2", "d2", "d2"), quad, keep_a)
    column = stack(quad, column, [h["u3"]])
    other = in_core(column)
    keep_b, send_b = partials(*mixed)
    got_b = in_core(send_b)
    token = phase(("u4", "dx3", "ux2"), ("u3", "dx2", "u2"), column, got_a, keep_b)
    keep_c, send_c = partials(*last_early, in_core(token))
    got_c = in_core(send_c)
    early = place(
        at_early,
        scalars,
        [(keep_a, got_a), (keep_b, got_b), (keep_c, got_c)],
        VMEM_LIMIT,
        [],
    )
    phase(("ux3", "dx4", "dx1"), ("ux2", "dx3", "d1"), other, *early)
    early = over_y(early)
    groups = [[h[s] for s in group] for group in last]
    got_d = in_core(chosen_sums(False, scalars, weight, groups, []))
    keep_d = chosen_sums(True, scalars, weight, groups, [])
    late = place(
        at_late,
        scalars,
        [(keep_b, got_b), (keep_d, got_d)],
        TAIL_LIMIT,
        early[1:],
    )

    grad_weight, token = weight_sums(
        at_inputs,
        scalars,
        column,
        other,
        [h[s] for s in order],
        1.0 / (Y * XH * C * rows),
        late,
    )

    keep, send = merge(at_here, scalars, over_y(late), early, [token])
    grad_in = (keep + in_xh(send)).astype(jnp.bfloat16)
    return grad_in.T, grad_weight


def solution(mesh):
    return jax.shard_map(
        body,
        mesh=mesh,
        in_specs=(P("gx", "gy"), P("gy", "gx"), P("gx", "gy")),
        out_specs=(P("gy", "gx"), P("gx", "gy")),
        check_vma=False,
    )
```

```python
import functools

import jax
import jax.numpy as jnp
from jax import lax
from jax.experimental import pallas as pl
from jax.experimental.pallas import tpu as pltpu
from jax.sharding import PartitionSpec as P

XL, Z = 2, 8
Y, XH, C = 4, 2, 2
VMEM_LIMIT = 127 << 19
TAIL_LIMIT = 32 << 20
NO_COST = pl.CostEstimate(flops=1, bytes_accessed=1, transcendentals=0)


def gx_pairs(dxl, dz):
    return [
        (xl * Z + z, (xl + dxl) % XL * Z + (z + dz) % Z)
        for xl in range(XL)
        for z in range(Z)
    ]


def gy_pairs(dy, dxh, dc):
    return [
        (
            (y * XH + xh) * C + c,
            ((y + dy) % Y * XH + (xh + dxh) % XH) * C + (c + dc) % C,
        )
        for y in range(Y)
        for xh in range(XH)
        for c in range(C)
    ]


def up(t):
    return lax.ppermute(t, "gx", gx_pairs(0, 1))


def down(t):
    return lax.ppermute(t, "gx", gx_pairs(0, -1))


def across(t):
    return lax.ppermute(t, "gx", gx_pairs(1, 0))


def in_y_pair(t):
    pairs = [
        ((y * XH + xh) * C + c, ((y ^ 1) * XH + xh) * C + c)
        for y in range(Y)
        for xh in range(XH)
        for c in range(C)
    ]
    return lax.ppermute(t, "gy", pairs)


def in_y(t, dy):
    return lax.ppermute(t, "gy", gy_pairs(dy, 0, 0))


def in_xh(t):
    return lax.ppermute(t, "gy", gy_pairs(0, 1, 0))


def late_here(z, xh, c):
    return (z + (z % 2 != c)) // 2 % 2 == xh


def in_core(t):
    return lax.ppermute(t, "gy", gy_pairs(0, 0, 1))


IN_HBM = pl.BlockSpec(memory_space=pltpu.HBM)
ANYWHERE = pl.BlockSpec(memory_space=pl.ANY)
VECTOR = pl.BlockSpec(memory_space=pltpu.VMEM)
SCALAR = pl.BlockSpec(memory_space=pltpu.SMEM)


def params(limit=VMEM_LIMIT):
    return pltpu.CompilerParams(vmem_limit_bytes=limit)


def tie_kernel(n, *refs):
    for token_ref in refs[n:]:
        token_ref[...] = jnp.zeros_like(token_ref)


def tie(values, after, tokens):
    n = len(values)
    return pl.pallas_call(
        functools.partial(tie_kernel, 2 * n + len(after)),
        out_shape=[jax.ShapeDtypeStruct(v.shape, v.dtype) for v in values]
        + [jax.ShapeDtypeStruct((8, 128), jnp.float32)] * tokens,
        in_specs=[IN_HBM] * n + [ANYWHERE] * len(after),
        out_specs=[IN_HBM] * n + [VECTOR] * tokens,
        input_output_aliases={k: k for k in range(n)},
        compiler_params=params(),
        cost_estimate=NO_COST,
        name="tie",
    )(*values, *after)


def touch_kernel(a_ref, out_ref):
    out_ref[...] = a_ref[...]


def touch(a):
    return pl.pallas_call(
        touch_kernel,
        out_shape=jax.ShapeDtypeStruct(a.shape, a.dtype),
        in_specs=[VECTOR],
        out_specs=VECTOR,
        compiler_params=params(),
        cost_estimate=NO_COST,
        name="touch",
    )(a)


def stack_kernel(a_ref, b_ref, *refs):
    n = a_ref.shape[0]
    refs[-1][:n] = a_ref[...]
    refs[-1][n:] = b_ref[...]


def stack(a, b, after):
    return pl.pallas_call(
        stack_kernel,
        out_shape=jax.ShapeDtypeStruct((2 * a.shape[0],) + a.shape[1:], a.dtype),
        in_specs=[VECTOR] * 2 + [ANYWHERE] * len(after),
        out_specs=VECTOR,
        compiler_params=params(),
        cost_estimate=NO_COST,
        name="stack",
    )(a, b, *after)


PARTS = 4


def load_weight(w_any, w_ref, sem, first):
    part = w_ref.shape[0] // PARTS
    copies = []
    for k in range(PARTS):
        rows = pl.ds(k * part, part)
        copy = pltpu.make_async_copy(
            w_any.at[rows, :], w_ref.at[rows, :], sem.at[first + k]
        )
        copy.start()
        copies.append(copy)
    return copies


def product(w_ref, g_ref):
    return lax.dot_general(
        w_ref[...],
        g_ref[...],
        (((1,), (1,)), ((), ())),
        preferred_element_type=jnp.float32,
    )


def partial_kernel(places, s_ref, w_any, *refs):
    n = len(places)
    pieces = refs[:n]
    keep_ref, send_ref, w_ref, g_ref, sem = refs[-5:]
    rows = keep_ref.shape[2]
    copies = load_weight(w_any, w_ref, sem, n)
    for k in range(n):
        copy = pltpu.make_async_copy(
            pieces[k], g_ref.at[pl.ds(k * rows, rows), :], sem.at[k]
        )
        copy.start()
        copies.append(copy)
    for copy in copies:
        copy.wait()
    sums = product(w_ref, g_ref)
    for k in range(n):
        group, slot = places[k]
        value = sums[:, k * rows : (k + 1) * rows]

        @pl.when(s_ref[0] == 1 - group)
        def _(slot=slot, value=value):
            keep_ref[slot] = value

        @pl.when(s_ref[0] == group)
        def _(slot=slot, value=value):
            send_ref[slot] = value


def partial_sums(first, weight, groups, after):
    places = [(g, k) for g, shards in enumerate(groups) for k in range(len(shards))]
    shards = [s for group in groups for s in group]
    n, slots = len(shards), max(len(group) for group in groups)
    rows, cols = shards[0].shape
    width = weight.shape[0]
    out = jax.ShapeDtypeStruct((slots, width, rows), jnp.float32)
    return pl.pallas_call(
        functools.partial(partial_kernel, places),
        out_shape=(out, out),
        in_specs=[SCALAR] + [IN_HBM] * (1 + n) + [ANYWHERE] * len(after),
        out_specs=(VECTOR, VECTOR),
        scratch_shapes=[
            pltpu.VMEM((width, cols), jnp.bfloat16),
            pltpu.VMEM((n * rows, cols), jnp.bfloat16),
            pltpu.SemaphoreType.DMA((n + PARTS,)),
        ],
        compiler_params=params(),
        cost_estimate=NO_COST,
        name="partial_sums",
    )(first, weight, *shards, *after)


def chosen_kernel(n, own, s_ref, w_any, *refs):
    out_ref, w_ref, g_ref, sem = refs[-4:]
    rows = out_ref.shape[2]
    copies = load_weight(w_any, w_ref, sem, n)
    for k in range(n):
        target = g_ref.at[pl.ds(k * rows, rows), :]
        for group in range(2):

            @pl.when((s_ref[0] == 1 - group) == own)
            def _(source=refs[group * n + k], target=target, k=k):
                pltpu.make_async_copy(source, target, sem.at[k]).start()

        copies.append(pltpu.make_async_copy(refs[k], target, sem.at[k]))
    for copy in copies:
        copy.wait()
    sums = product(w_ref, g_ref)
    for k in range(n):
        out_ref[k] = sums[:, k * rows : (k + 1) * rows]


def chosen_sums(own, scalars, weight, groups, after):
    n = len(groups[0])
    rows, cols = groups[0][0].shape
    width = weight.shape[0]
    return pl.pallas_call(
        functools.partial(chosen_kernel, n, own),
        out_shape=jax.ShapeDtypeStruct((n, width, rows), jnp.float32),
        in_specs=[SCALAR] + [IN_HBM] * (1 + 2 * n) + [ANYWHERE] * len(after),
        out_specs=VECTOR,
        scratch_shapes=[
            pltpu.VMEM((width, cols), jnp.bfloat16),
            pltpu.VMEM((n * rows, cols), jnp.bfloat16),
            pltpu.SemaphoreType.DMA((n + PARTS,)),
        ],
        compiler_params=params(),
        cost_estimate=NO_COST,
        name="chosen_sums",
    )(scalars, weight, *groups[0], *groups[1], *after)


def place_kernel(base, counts, s_ref, *refs):
    pairs, outs = refs[: 2 * len(counts)], refs[-Y:]
    k = base
    for group, n in enumerate(counts):
        keep_ref, got_ref = pairs[2 * group], pairs[2 * group + 1]
        for i in range(n):
            for r, out_ref in enumerate(outs):

                @pl.when(s_ref[k] == r)
                def _(keep_ref=keep_ref, got_ref=got_ref, i=i, out_ref=out_ref):
                    out_ref[...] = keep_ref[i] + got_ref[i]

            k += 1


def place(base, scalars, groups, limit, after):
    counts = [kept.shape[0] for kept, _ in groups]
    out = jax.ShapeDtypeStruct(groups[0][0].shape[1:], jnp.float32)
    return pl.pallas_call(
        functools.partial(place_kernel, base, counts),
        out_shape=[out] * Y,
        in_specs=[SCALAR] + [VECTOR] * (2 * len(counts)) + [ANYWHERE] * len(after),
        out_specs=[VECTOR] * Y,
        compiler_params=params(limit),
        cost_estimate=NO_COST,
        name="place",
    )(scalars, *[a for pair in groups for a in pair], *after)


def merge_kernel(base, s_ref, *refs):
    late, early, (keep_ref, send_ref) = refs[:Y], refs[Y : 2 * Y], refs[-2:]

    def total(parts):
        return (parts[0][...] + parts[1][...]) + (parts[2][...] + parts[3][...])

    a, b = total(late), total(early)
    here = s_ref[base] == 1
    keep_ref[...] = jnp.where(here, a, b)
    send_ref[...] = jnp.where(here, b, a)


def merge(base, scalars, late, early, after):
    out = jax.ShapeDtypeStruct(late[0].shape, jnp.float32)
    return pl.pallas_call(
        functools.partial(merge_kernel, base),
        out_shape=(out, out),
        in_specs=[SCALAR] + [VECTOR] * (2 * Y) + [ANYWHERE] * len(after),
        out_specs=(VECTOR, VECTOR),
        compiler_params=params(TAIL_LIMIT),
        cost_estimate=NO_COST,
        name="merge",
    )(scalars, *late, *early, *after)


def weight_kernel(base, n, tile, scale, s_ref, mine_ref, other_ref, *refs):
    pieces, (out_ref, token_ref) = refs[:n], refs[-7:-5]
    x_ref, g_ref, o_ref, in_sem, out_sem = refs[-5:]
    count, _, rows = mine_ref.shape
    copies = []
    for k in range(n):
        copy = pltpu.make_async_copy(
            pieces[k], g_ref.at[pl.ds(k * rows, rows), :], in_sem.at[k]
        )
        copy.start()
        copies.append(copy)
    token_ref[...] = jnp.zeros_like(token_ref)
    for k in range(n):
        at = s_ref[base + k]
        here = slice(k * rows, (k + 1) * rows)

        @pl.when(at < count)
        def _(at=at, here=here):
            x_ref[:, here] = mine_ref[jnp.minimum(at, count - 1)]

        @pl.when(at >= count)
        def _(at=at, here=here):
            x_ref[:, here] = other_ref[jnp.maximum(at - count, 0)]

    for copy in copies:
        copy.wait()
    results = []
    for t in range(g_ref.shape[1] // tile):
        columns = slice(t * tile, (t + 1) * tile)
        product = jnp.dot(
            x_ref[...], g_ref[:, columns], preferred_element_type=jnp.float32
        )
        o_ref[:, columns] = product * scale
        copy = pltpu.make_async_copy(
            o_ref.at[:, columns], out_ref.at[:, columns], out_sem.at[t]
        )
        copy.start()
        results.append(copy)
    for copy in results:
        copy.wait()


def weight_sums(base, scalars, mine, other, shards, scale, after):
    n = len(shards)
    rows, cols = shards[0].shape
    width = mine.shape[1]
    tile = 768
    return pl.pallas_call(
        functools.partial(weight_kernel, base, n, tile, scale),
        out_shape=(
            jax.ShapeDtypeStruct((width, cols), jnp.float32),
            jax.ShapeDtypeStruct((8, 128), jnp.float32),
        ),
        in_specs=[SCALAR, VECTOR, VECTOR] + [IN_HBM] * n + [ANYWHERE] * len(after),
        out_specs=(IN_HBM, VECTOR),
        scratch_shapes=[
            pltpu.VMEM((width, n * rows), jnp.bfloat16),
            pltpu.VMEM((n * rows, cols), jnp.bfloat16),
            pltpu.VMEM((width, cols), jnp.float32),
            pltpu.SemaphoreType.DMA((n,)),
            pltpu.SemaphoreType.DMA((cols // tile,)),
        ],
        compiler_params=params(),
        cost_estimate=NO_COST,
        name="weight_sums",
    )(scalars, mine, other, *shards, *after)


def body(grad_out, inputs, weight):
    ix, iy = lax.axis_index("gx"), lax.axis_index("gy")
    xl, z = ix // Z, ix % Z
    y, xh, c = iy // (XH * C), iy // C % XH, iy % C
    rows = grad_out.shape[0]

    at = {"g": (0, 0), "gx": (1, 0)}
    for k in range(1, 5):
        at[f"u{k}"], at[f"ux{k}"] = (0, -k), (1, -k)
        at[f"d{k}"], at[f"dx{k}"] = (0, k), (1, k)

    def where(name):
        side, dz = at[name]
        x = xl if side == 0 else 1 - xl
        place = (z + dz) % Z
        return x * 2 + place // 4, place // 2 % 2, place % 2

    sets = (
        ("g", "gx", "u4", "dx4"),
        ("d1", "dx1", "u3", "ux3"),
        ("d2", "dx2", "u2", "ux2"),
        ("d3", "dx3", "u1", "ux1"),
    )
    even = z % 2 == c
    h = {"g": grad_out}

    first_early = (("d2", "u2"), ("u1", "ux1"))
    mixed = (("dx2", "g", "gx"), ("d3", "d1", "u3"))
    last_early = (("ux2",), ("dx3",))
    last = (("u4", "dx4"), ("dx1", "ux3"))
    order = [s for names in sets for s in names]

    def ways(*groups):
        slots = []
        for a, b in groups:
            for k in range(max(len(a), len(b), 1)):
                way = [(where(s[k])[0] - y) % Y if k < len(s) else -1 for s in (a, b)]
                slots.append(jnp.where(even, way[0], way[1]))
        return slots

    def of_inputs(name):
        ty, txh, tc = where(name)
        k = (ty // 2 != y // 2) * 4 + (ty % 2 != y % 2) * 2 + (txh != xh)
        return jnp.where(tc == c, k, k + Y * XH)

    none = ((), ())
    lists = [
        [even],
        ways(first_early, (mixed[0][:1], mixed[1][:1]), none, none, last_early),
        ways(none, (mixed[0][1:], mixed[1][1:]), last),
        [of_inputs(s) for s in order],
        [late_here(z, xh, c)],
    ]
    scalars = jnp.stack([jnp.int32(v) for values in lists for v in values])
    _, at_early, at_late, at_inputs, at_here = (
        sum(len(values) for values in lists[:k]) for k in range(len(lists))
    )

    def partials(a, b, *after):
        groups = [h[s] for s in a], [h[s] for s in b]
        return partial_sums(scalars, weight, groups, after)

    def over_y(parts):
        return [parts[0], in_y(parts[1], 1), in_y(parts[3], -1), in_y(parts[2], 2)]

    def phase(names, sends, *after, tokens=0):
        s = [h[name] for name in sends]
        got = tie([up(s[0]), down(s[1]), across(s[2])], after, tokens)
        h.update(zip(names, got))
        return got[3:]

    mine = touch(inputs.T[None])
    pair = in_xh(mine)
    phase(("u1", "d1", "gx"), ("g", "g", "g"), pair)
    pair = stack(mine, pair, [h["u1"]])
    quad = in_y_pair(pair)
    phase(("u2", "d2", "ux1"), ("u1", "d1", "u1"), pair)
    quad = stack(pair, quad, [h["u2"]])
    column = in_y(quad, 2)
    keep_a, send_a = partials(*first_early)
    got_a = in_core(send_a)
    phase(("u3", "d3", "dx2"), ("u2", "d2", "d2"), quad, keep_a)
    column = stack(quad, column, [h["u3"]])
    other = in_core(column)
    keep_b, send_b = partials(*mixed)
    got_b = in_core(send_b)
    (token,) = phase(
        ("u4", "dx3", "ux2"), ("u3", "dx2", "u2"), column, got_a, keep_b, tokens=1
    )
    keep_c, send_c = partials(*last_early, in_core(token), other)
    got_c = in_core(send_c)
    early = place(
        at_early,
        scalars,
        [(keep_a, got_a), (keep_b, got_b), (keep_c, got_c)],
        VMEM_LIMIT,
        [],
    )
    phase(("ux3", "dx4", "dx1"), ("ux2", "dx3", "d1"), other, *early)
    early = over_y(early)
    groups = [[h[s] for s in group] for group in last]
    got_d = in_core(chosen_sums(False, scalars, weight, groups, []))
    keep_d = chosen_sums(True, scalars, weight, groups, [])
    late = place(
        at_late,
        scalars,
        [(keep_b, got_b), (keep_d, got_d)],
        VMEM_LIMIT,
        [],
    )

    grad_weight, token = weight_sums(
        at_inputs,
        scalars,
        column,
        other,
        [h[s] for s in order],
        1.0 / (Y * XH * C * rows),
        late,
    )

    keep, send = merge(at_here, scalars, over_y(late), early, [token])
    grad_in = (keep + in_xh(send)).astype(jnp.bfloat16)
    return grad_in.T, grad_weight


def solution(mesh):
    return jax.shard_map(
        body,
        mesh=mesh,
        in_specs=(P("gx", "gy"), P("gy", "gx"), P("gx", "gy")),
        out_specs=(P("gy", "gx"), P("gx", "gy")),
        check_vma=False,
    )
```

```python
import functools

import jax
import jax.numpy as jnp
from jax import lax
from jax.experimental import pallas as pl
from jax.experimental.pallas import tpu as pltpu
from jax.sharding import PartitionSpec as P

XL, Z = 2, 8
Y, XH, C = 4, 2, 2
VMEM_LIMIT = 127 << 19
NO_COST = pl.CostEstimate(flops=1, bytes_accessed=1, transcendentals=0)


def gx_pairs(dxl, dz):
    return [
        (xl * Z + z, (xl + dxl) % XL * Z + (z + dz) % Z)
        for xl in range(XL)
        for z in range(Z)
    ]


def gy_pairs(dy, dxh, dc):
    return [
        (
            (y * XH + xh) * C + c,
            ((y + dy) % Y * XH + (xh + dxh) % XH) * C + (c + dc) % C,
        )
        for y in range(Y)
        for xh in range(XH)
        for c in range(C)
    ]


def up(t):
    return lax.ppermute(t, "gx", gx_pairs(0, 1))


def down(t):
    return lax.ppermute(t, "gx", gx_pairs(0, -1))


def across(t):
    return lax.ppermute(t, "gx", gx_pairs(1, 0))


def in_y_pair(t):
    pairs = [
        ((y * XH + xh) * C + c, ((y ^ 1) * XH + xh) * C + c)
        for y in range(Y)
        for xh in range(XH)
        for c in range(C)
    ]
    return lax.ppermute(t, "gy", pairs)


def in_y(t, dy):
    return lax.ppermute(t, "gy", gy_pairs(dy, 0, 0))


def in_xh(t):
    return lax.ppermute(t, "gy", gy_pairs(0, 1, 0))


def in_core(t):
    return lax.ppermute(t, "gy", gy_pairs(0, 0, 1))


AT = {"g": (0, 0), "gx": (1, 0)}
for _k in range(1, 5):
    AT[f"u{_k}"], AT[f"ux{_k}"] = (0, -_k), (1, -_k)
    AT[f"d{_k}"], AT[f"dx{_k}"] = (0, _k), (1, _k)


def position():
    ix, iy = lax.axis_index("gx"), lax.axis_index("gy")
    return ix >> 3, ix & 7, iy >> 2, (iy >> 1) & 1, iy & 1


def where(here, name):
    side, dz = AT[name]
    at = (here[1] + dz + Z) & 7
    return (here[0] ^ side) * 2 + (at >> 2), (at >> 1) & 1, at & 1


def keeps_even(here):
    return (here[1] & 1) == here[4]


def way(here, name):
    return (where(here, name)[0] - here[2]) & 3


def of_inputs(here, name):
    y, xh, c = where(here, name)
    dy = y ^ here[2]
    return (c ^ here[4]) * 8 + (dy >> 1) * 4 + (dy & 1) * 2 + (xh ^ here[3])


def ends_late(here):
    _, z, _, xh, c = here
    return ((z + ((z & 1) ^ c)) >> 1) & 1 == xh


IN_HBM = pl.BlockSpec(memory_space=pltpu.HBM)
ANYWHERE = pl.BlockSpec(memory_space=pl.ANY)
VECTOR = pl.BlockSpec(memory_space=pltpu.VMEM)


def params():
    return pltpu.CompilerParams(vmem_limit_bytes=VMEM_LIMIT)


def tie_kernel(n, *refs):
    for token_ref in refs[n:]:
        token_ref[...] = jnp.zeros_like(token_ref)


def tie(values, after, tokens):
    n = len(values)
    return pl.pallas_call(
        functools.partial(tie_kernel, 2 * n + len(after)),
        out_shape=[jax.ShapeDtypeStruct(v.shape, v.dtype) for v in values]
        + [jax.ShapeDtypeStruct((8, 128), jnp.float32)] * tokens,
        in_specs=[IN_HBM] * n + [ANYWHERE] * len(after),
        out_specs=[IN_HBM] * n + [VECTOR] * tokens,
        input_output_aliases={k: k for k in range(n)},
        compiler_params=params(),
        cost_estimate=NO_COST,
        name="tie",
    )(*values, *after)


def touch_kernel(a_ref, out_ref):
    out_ref[...] = a_ref[...]


def touch(a):
    return pl.pallas_call(
        touch_kernel,
        out_shape=jax.ShapeDtypeStruct(a.shape, a.dtype),
        in_specs=[VECTOR],
        out_specs=VECTOR,
        compiler_params=params(),
        cost_estimate=NO_COST,
        name="touch",
    )(a)


def stack_kernel(a_ref, b_ref, *refs):
    n = a_ref.shape[0]
    refs[-1][:n] = a_ref[...]
    refs[-1][n:] = b_ref[...]


def stack(a, b, after):
    return pl.pallas_call(
        stack_kernel,
        out_shape=jax.ShapeDtypeStruct((2 * a.shape[0],) + a.shape[1:], a.dtype),
        in_specs=[VECTOR] * 2 + [ANYWHERE] * len(after),
        out_specs=VECTOR,
        compiler_params=params(),
        cost_estimate=NO_COST,
        name="stack",
    )(a, b, *after)


PARTS = 4


def load_weight(w_any, w_ref, sem, first):
    part = w_ref.shape[0] // PARTS
    copies = []
    for k in range(PARTS):
        rows = pl.ds(k * part, part)
        copy = pltpu.make_async_copy(
            w_any.at[rows, :], w_ref.at[rows, :], sem.at[first + k]
        )
        copy.start()
        copies.append(copy)
    return copies


def product(w_ref, g_ref):
    return lax.dot_general(
        w_ref[...],
        g_ref[...],
        (((1,), (1,)), ((), ())),
        preferred_element_type=jnp.float32,
    )


def partial_kernel(places, w_any, *refs):
    n = len(places)
    pieces = refs[:n]
    keep_ref, send_ref, w_ref, g_ref, sem = refs[-5:]
    rows = keep_ref.shape[2]
    copies = load_weight(w_any, w_ref, sem, n)
    for k in range(n):
        copy = pltpu.make_async_copy(
            pieces[k], g_ref.at[pl.ds(k * rows, rows), :], sem.at[k]
        )
        copy.start()
        copies.append(copy)
    even = keeps_even(position())
    for copy in copies:
        copy.wait()
    sums = product(w_ref, g_ref)
    for k in range(n):
        group, slot = places[k]
        value = sums[:, k * rows : (k + 1) * rows]

        @pl.when(even == (group == 0))
        def _(slot=slot, value=value):
            keep_ref[slot] = value

        @pl.when(even == (group == 1))
        def _(slot=slot, value=value):
            send_ref[slot] = value


def partial_sums(weight, groups, after):
    places = [(g, k) for g, shards in enumerate(groups) for k in range(len(shards))]
    shards = [s for group in groups for s in group]
    n, slots = len(shards), max(len(group) for group in groups)
    rows, cols = shards[0].shape
    width = weight.shape[0]
    out = jax.ShapeDtypeStruct((slots, width, rows), jnp.float32)
    return pl.pallas_call(
        functools.partial(partial_kernel, places),
        out_shape=(out, out),
        in_specs=[IN_HBM] * (1 + n) + [ANYWHERE] * len(after),
        out_specs=(VECTOR, VECTOR),
        scratch_shapes=[
            pltpu.VMEM((width, cols), jnp.bfloat16),
            pltpu.VMEM((n * rows, cols), jnp.bfloat16),
            pltpu.SemaphoreType.DMA((n + PARTS,)),
        ],
        compiler_params=params(),
        cost_estimate=NO_COST,
        name="partial_sums",
    )(weight, *shards, *after)


def place_kernel(groups, *refs):
    pairs, outs = refs[: 2 * len(groups)], refs[-Y:]
    here = position()
    even = keeps_even(here)
    for group, slots in enumerate(groups):
        keep_ref, got_ref = pairs[2 * group], pairs[2 * group + 1]
        for i, names in slots:
            to = [-1 if name is None else way(here, name) for name in names]
            to = jnp.where(even, to[0], to[1])
            for r, out_ref in enumerate(outs):

                @pl.when(to == r)
                def _(keep_ref=keep_ref, got_ref=got_ref, i=i, out_ref=out_ref):
                    out_ref[...] = keep_ref[i] + got_ref[i]


def place(groups):
    arrays = [a for kept, got, _ in groups for a in (kept, got)]
    out = jax.ShapeDtypeStruct(arrays[0].shape[1:], jnp.float32)
    return pl.pallas_call(
        functools.partial(place_kernel, [slots for _, _, slots in groups]),
        out_shape=[out] * Y,
        in_specs=[VECTOR] * len(arrays),
        out_specs=[VECTOR] * Y,
        compiler_params=params(),
        cost_estimate=NO_COST,
        name="place",
    )(*arrays)


def merge_kernel(*refs):
    late, early, (keep_ref, send_ref) = refs[:Y], refs[Y : 2 * Y], refs[-2:]

    def total(parts):
        return (parts[0][...] + parts[1][...]) + (parts[2][...] + parts[3][...])

    a, b = total(late), total(early)
    here = ends_late(position())
    keep_ref[...] = jnp.where(here, a, b)
    send_ref[...] = jnp.where(here, b, a)


def merge(late, early, after):
    out = jax.ShapeDtypeStruct(late[0].shape, jnp.float32)
    return pl.pallas_call(
        merge_kernel,
        out_shape=(out, out),
        in_specs=[VECTOR] * (2 * Y) + [ANYWHERE] * len(after),
        out_specs=(VECTOR, VECTOR),
        compiler_params=params(),
        cost_estimate=NO_COST,
        name="merge",
    )(*late, *early, *after)


def weight_kernel(names, tile, scale, mine_ref, other_ref, *refs):
    n = len(names)
    pieces, (out_ref, token_ref) = refs[:n], refs[-7:-5]
    x_ref, g_ref, o_ref, in_sem, out_sem = refs[-5:]
    count, _, rows = mine_ref.shape
    tiles = g_ref.shape[1] // tile
    copies = []
    for t in range(tiles):
        columns = pl.ds(t * tile, tile)
        for k in range(n):
            copy = pltpu.make_async_copy(
                pieces[k].at[:, columns],
                g_ref.at[pl.ds(k * rows, rows), columns],
                in_sem.at[t * n + k],
            )
            copy.start()
            copies.append(copy)
    token_ref[...] = jnp.zeros_like(token_ref)
    here = position()
    for k, name in enumerate(names):
        at = of_inputs(here, name)
        target = slice(k * rows, (k + 1) * rows)

        @pl.when(at < count)
        def _(at=at, target=target):
            x_ref[:, target] = mine_ref[jnp.minimum(at, count - 1)]

        @pl.when(at >= count)
        def _(at=at, target=target):
            x_ref[:, target] = other_ref[jnp.maximum(at - count, 0)]

    results = []
    for t in range(tiles):
        columns = slice(t * tile, (t + 1) * tile)
        for copy in copies[t * n : (t + 1) * n]:
            copy.wait()
        sums = jnp.dot(
            x_ref[...], g_ref[:, columns], preferred_element_type=jnp.float32
        )
        o_ref[:, columns] = sums * scale
        copy = pltpu.make_async_copy(
            o_ref.at[:, columns], out_ref.at[:, columns], out_sem.at[t]
        )
        copy.start()
        results.append(copy)
    for copy in results:
        copy.wait()


def weight_sums(names, mine, other, shards, scale, after):
    n = len(shards)
    rows, cols = shards[0].shape
    width = mine.shape[1]
    tile = 768
    return pl.pallas_call(
        functools.partial(weight_kernel, names, tile, scale),
        out_shape=(
            jax.ShapeDtypeStruct((width, cols), jnp.float32),
            jax.ShapeDtypeStruct((8, 128), jnp.float32),
        ),
        in_specs=[VECTOR, VECTOR] + [IN_HBM] * n + [ANYWHERE] * len(after),
        out_specs=(IN_HBM, VECTOR),
        scratch_shapes=[
            pltpu.VMEM((width, n * rows), jnp.bfloat16),
            pltpu.VMEM((n * rows, cols), jnp.bfloat16),
            pltpu.VMEM((width, cols), jnp.float32),
            pltpu.SemaphoreType.DMA((n * (cols // tile),)),
            pltpu.SemaphoreType.DMA((cols // tile,)),
        ],
        compiler_params=params(),
        cost_estimate=NO_COST,
        name="weight_sums",
    )(mine, other, *shards, *after)


def body(grad_out, inputs, weight):
    rows = grad_out.shape[0]
    h = {"g": grad_out}

    first_early = (("d2", "u2"), ("u1", "ux1"))
    mixed = (("dx2", "g", "gx"), ("d3", "d1", "u3"))
    last_early = (("ux2",), ("dx3",))
    last = (("u4", "dx4"), ("dx1", "ux3"))

    def partials(groups, *after):
        return partial_sums(weight, [[h[s] for s in group] for group in groups], after)

    def slots(groups, *chosen):
        return [(k, (groups[0][k], groups[1][k])) for k in chosen]

    def over_y(parts):
        return [parts[0], in_y(parts[1], 1), in_y(parts[3], -1), in_y(parts[2], 2)]

    def phase(names, sends, *after, tokens=0):
        s = [h[name] for name in sends]
        got = tie([up(s[0]), down(s[1]), across(s[2])], after, tokens)
        h.update(zip(names, got))
        return got[3:]

    mine = touch(inputs.T[None])
    pair = in_xh(mine)
    phase(("u1", "d1", "gx"), ("g", "g", "g"), pair)
    pair = stack(mine, pair, [h["u1"]])
    quad = in_y_pair(pair)
    phase(("u2", "d2", "ux1"), ("u1", "d1", "u1"), pair)
    quad = stack(pair, quad, [h["u2"]])
    column = in_y(quad, 2)
    keep_a, send_a = partials(first_early)
    got_a = in_core(send_a)
    phase(("u3", "d3", "dx2"), ("u2", "d2", "d2"), quad, keep_a)
    column = stack(quad, column, [h["u3"]])
    other = in_core(column)
    keep_b, send_b = partials(mixed)
    got_b = in_core(send_b)
    (token,) = phase(
        ("u4", "dx3", "ux2"), ("u3", "dx2", "u2"), column, got_a, keep_b, tokens=1
    )
    keep_c, send_c = partials(last_early, in_core(token))
    got_c = in_core(send_c)
    early = place(
        [
            (keep_a, got_a, slots(first_early, 0, 1)),
            (keep_b, got_b, slots(mixed, 0)),
            (keep_c, got_c, slots(last_early, 0)),
        ]
    )
    phase(("ux3", "dx4", "dx1"), ("ux2", "dx3", "d1"), other, *early)
    early = over_y(early)
    keep_d, send_d = partials(last)
    got_d = in_core(send_d)
    late = place(
        [(keep_b, got_b, slots(mixed, 1, 2)), (keep_d, got_d, slots(last, 0, 1))]
    )

    order = [s for groups in (first_early, mixed, last_early, last) for group in groups for s in group]
    grad_weight, token = weight_sums(
        order,
        column,
        other,
        [h[s] for s in order],
        1.0 / (Y * XH * C * rows),
        late,
    )

    keep, send = merge(over_y(late), early, [token])
    grad_in = (keep + in_xh(send)).astype(jnp.bfloat16)
    return grad_in.T, grad_weight


def solution(mesh):
    return jax.shard_map(
        body,
        mesh=mesh,
        in_specs=(P("gx", "gy"), P("gy", "gx"), P("gx", "gy")),
        out_specs=(P("gy", "gx"), P("gx", "gy")),
        check_vma=False,
    )
```

```python
import functools

import jax
import jax.numpy as jnp
from jax import lax
from jax.experimental import pallas as pl
from jax.experimental.pallas import tpu as pltpu
from jax.sharding import PartitionSpec as P

XL, Z = 2, 8
Y, XH, C = 4, 2, 2
VMEM_LIMIT = 127 << 19
NO_COST = pl.CostEstimate(flops=1, bytes_accessed=1, transcendentals=0)


def gx_pairs(dxl, dz):
    return [
        (xl * Z + z, (xl + dxl) % XL * Z + (z + dz) % Z)
        for xl in range(XL)
        for z in range(Z)
    ]


def gy_pairs(dy, dxh, dc):
    return [
        (
            (y * XH + xh) * C + c,
            ((y + dy) % Y * XH + (xh + dxh) % XH) * C + (c + dc) % C,
        )
        for y in range(Y)
        for xh in range(XH)
        for c in range(C)
    ]


def up(t):
    return lax.ppermute(t, "gx", gx_pairs(0, 1))


def down(t):
    return lax.ppermute(t, "gx", gx_pairs(0, -1))


def across(t):
    return lax.ppermute(t, "gx", gx_pairs(1, 0))


def in_y_pair(t):
    pairs = [
        ((y * XH + xh) * C + c, ((y ^ 1) * XH + xh) * C + c)
        for y in range(Y)
        for xh in range(XH)
        for c in range(C)
    ]
    return lax.ppermute(t, "gy", pairs)


def in_y(t, dy):
    return lax.ppermute(t, "gy", gy_pairs(dy, 0, 0))


def in_xh(t):
    return lax.ppermute(t, "gy", gy_pairs(0, 1, 0))


def in_core(t):
    return lax.ppermute(t, "gy", gy_pairs(0, 0, 1))


AT = {"g": (0, 0), "gx": (1, 0)}
for _k in range(1, 5):
    AT[f"u{_k}"], AT[f"ux{_k}"] = (0, -_k), (1, -_k)
    AT[f"d{_k}"], AT[f"dx{_k}"] = (0, _k), (1, _k)


def position():
    ix, iy = lax.axis_index("gx"), lax.axis_index("gy")
    return ix >> 3, ix & 7, iy >> 2, (iy >> 1) & 1, iy & 1


def where(here, name):
    side, dz = AT[name]
    at = (here[1] + dz + Z) & 7
    return (here[0] ^ side) * 2 + (at >> 2), (at >> 1) & 1, at & 1


def keeps_even(here):
    return (here[1] & 1) == here[4]


def way(here, name):
    return (where(here, name)[0] - here[2]) & 3


def of_inputs(here, name):
    y, xh, c = where(here, name)
    dy = y ^ here[2]
    return (c ^ here[4]) * 8 + (dy >> 1) * 4 + (dy & 1) * 2 + (xh ^ here[3])


def ends_late(here):
    _, z, _, xh, c = here
    return ((z + ((z & 1) ^ c)) >> 1) & 1 == xh


IN_HBM = pl.BlockSpec(memory_space=pltpu.HBM)
ANYWHERE = pl.BlockSpec(memory_space=pl.ANY)
VECTOR = pl.BlockSpec(memory_space=pltpu.VMEM)


def params():
    return pltpu.CompilerParams(vmem_limit_bytes=VMEM_LIMIT)


def tie_kernel(n, *refs):
    for token_ref in refs[n:]:
        token_ref[...] = jnp.zeros_like(token_ref)


def tie(values, after, tokens):
    n = len(values)
    return pl.pallas_call(
        functools.partial(tie_kernel, 2 * n + len(after)),
        out_shape=[jax.ShapeDtypeStruct(v.shape, v.dtype) for v in values]
        + [jax.ShapeDtypeStruct((8, 128), jnp.float32)] * tokens,
        in_specs=[IN_HBM] * n + [ANYWHERE] * len(after),
        out_specs=[IN_HBM] * n + [VECTOR] * tokens,
        input_output_aliases={k: k for k in range(n)},
        compiler_params=params(),
        cost_estimate=NO_COST,
        name="tie",
    )(*values, *after)


def touch_kernel(a_ref, out_ref):
    out_ref[...] = a_ref[...]


def touch(a):
    return pl.pallas_call(
        touch_kernel,
        out_shape=jax.ShapeDtypeStruct(a.shape, a.dtype),
        in_specs=[VECTOR],
        out_specs=VECTOR,
        compiler_params=params(),
        cost_estimate=NO_COST,
        name="touch",
    )(a)


def stack_kernel(a_ref, b_ref, *refs):
    n = a_ref.shape[0]
    refs[-1][:n] = a_ref[...]
    refs[-1][n:] = b_ref[...]


def stack(a, b, after):
    return pl.pallas_call(
        stack_kernel,
        out_shape=jax.ShapeDtypeStruct((2 * a.shape[0],) + a.shape[1:], a.dtype),
        in_specs=[VECTOR] * 2 + [ANYWHERE] * len(after),
        out_specs=VECTOR,
        compiler_params=params(),
        cost_estimate=NO_COST,
        name="stack",
    )(a, b, *after)


PARTS = 4


def load_weight(w_any, w_ref, sem, first):
    part = w_ref.shape[0] // PARTS
    copies = []
    for k in range(PARTS):
        rows = pl.ds(k * part, part)
        copy = pltpu.make_async_copy(
            w_any.at[rows, :], w_ref.at[rows, :], sem.at[first + k]
        )
        copy.start()
        copies.append(copy)
    return copies


def product(w_ref, g_ref):
    return lax.dot_general(
        w_ref[...],
        g_ref[...],
        (((1,), (1,)), ((), ())),
        preferred_element_type=jnp.float32,
    )


def partial_kernel(places, w_any, *refs):
    n = len(places)
    pieces = refs[:n]
    keep_ref, send_ref, w_ref, g_ref, sem = refs[-5:]
    rows = keep_ref.shape[2]
    copies = load_weight(w_any, w_ref, sem, n)
    for k in range(n):
        copy = pltpu.make_async_copy(
            pieces[k], g_ref.at[pl.ds(k * rows, rows), :], sem.at[k]
        )
        copy.start()
        copies.append(copy)
    even = keeps_even(position())
    for copy in copies:
        copy.wait()
    sums = product(w_ref, g_ref)
    for k in range(n):
        group, slot = places[k]
        value = sums[:, k * rows : (k + 1) * rows]

        @pl.when(even == (group == 0))
        def _(slot=slot, value=value):
            keep_ref[slot] = value

        @pl.when(even == (group == 1))
        def _(slot=slot, value=value):
            send_ref[slot] = value


def partial_sums(weight, groups, after):
    places = [(g, k) for g, shards in enumerate(groups) for k in range(len(shards))]
    shards = [s for group in groups for s in group]
    n, slots = len(shards), max(len(group) for group in groups)
    rows, cols = shards[0].shape
    width = weight.shape[0]
    out = jax.ShapeDtypeStruct((slots, width, rows), jnp.float32)
    return pl.pallas_call(
        functools.partial(partial_kernel, places),
        out_shape=(out, out),
        in_specs=[IN_HBM] * (1 + n) + [ANYWHERE] * len(after),
        out_specs=(VECTOR, VECTOR),
        scratch_shapes=[
            pltpu.VMEM((width, cols), jnp.bfloat16),
            pltpu.VMEM((n * rows, cols), jnp.bfloat16),
            pltpu.SemaphoreType.DMA((n + PARTS,)),
        ],
        compiler_params=params(),
        cost_estimate=NO_COST,
        name="partial_sums",
    )(weight, *shards, *after)


def place_kernel(groups, *refs):
    n = 2 * len(groups)
    pairs, outs = refs[:n], refs[-Y:]
    extra = refs[n : n + (len(refs) - n - Y) // 2]
    for k, extra_ref in enumerate(extra):
        refs[-Y - 1 - k][...] = extra_ref[...]
    here = position()
    even = keeps_even(here)
    for group, slots in enumerate(groups):
        keep_ref, got_ref = pairs[2 * group], pairs[2 * group + 1]
        for i, names in slots:
            to = [-1 if name is None else way(here, name) for name in names]
            to = jnp.where(even, to[0], to[1])
            for r, out_ref in enumerate(outs):

                @pl.when(to == r)
                def _(keep_ref=keep_ref, got_ref=got_ref, i=i, out_ref=out_ref):
                    out_ref[...] = keep_ref[i] + got_ref[i]


def place(groups, extra):
    arrays = [a for kept, got, _ in groups for a in (kept, got)]
    out = jax.ShapeDtypeStruct(arrays[0].shape[1:], jnp.float32)
    return pl.pallas_call(
        functools.partial(place_kernel, [slots for _, _, slots in groups]),
        out_shape=[out] * (len(extra) + Y),
        in_specs=[VECTOR] * (len(arrays) + len(extra)),
        out_specs=[VECTOR] * (len(extra) + Y),
        compiler_params=params(),
        cost_estimate=NO_COST,
        name="place",
    )(*arrays, *extra)


def merge_kernel(*refs):
    late, early, (keep_ref, send_ref) = refs[:Y], refs[Y : 2 * Y], refs[-2:]

    def total(parts):
        return (parts[0][...] + parts[1][...]) + (parts[2][...] + parts[3][...])

    a, b = total(late), total(early)
    here = ends_late(position())
    keep_ref[...] = jnp.where(here, a, b)
    send_ref[...] = jnp.where(here, b, a)


def merge(late, early, after):
    out = jax.ShapeDtypeStruct(late[0].shape, jnp.float32)
    return pl.pallas_call(
        merge_kernel,
        out_shape=(out, out),
        in_specs=[VECTOR] * (2 * Y) + [ANYWHERE] * len(after),
        out_specs=(VECTOR, VECTOR),
        compiler_params=params(),
        cost_estimate=NO_COST,
        name="merge",
    )(*late, *early, *after)


def weight_kernel(names, tile, scale, mine_ref, other_ref, *refs):
    n = len(names)
    pieces, (out_ref, token_ref) = refs[:n], refs[-7:-5]
    x_ref, g_ref, o_ref, in_sem, out_sem = refs[-5:]
    count, _, rows = mine_ref.shape
    tiles = g_ref.shape[1] // tile
    copies = []
    for t in range(tiles):
        columns = pl.ds(t * tile, tile)
        for k in range(n):
            copy = pltpu.make_async_copy(
                pieces[k].at[:, columns],
                g_ref.at[pl.ds(k * rows, rows), columns],
                in_sem.at[t * n + k],
            )
            copy.start()
            copies.append(copy)
    token_ref[...] = jnp.zeros_like(token_ref)
    here = position()
    for k, name in enumerate(names):
        at = of_inputs(here, name)
        target = slice(k * rows, (k + 1) * rows)

        @pl.when(at < count)
        def _(at=at, target=target):
            x_ref[:, target] = mine_ref[jnp.minimum(at, count - 1)]

        @pl.when(at >= count)
        def _(at=at, target=target):
            x_ref[:, target] = other_ref[jnp.maximum(at - count, 0)]

    results = []
    for t in range(tiles):
        columns = slice(t * tile, (t + 1) * tile)
        for copy in copies[t * n : (t + 1) * n]:
            copy.wait()
        sums = jnp.dot(
            x_ref[...], g_ref[:, columns], preferred_element_type=jnp.float32
        )
        o_ref[:, columns] = sums * scale
        copy = pltpu.make_async_copy(
            o_ref.at[:, columns], out_ref.at[:, columns], out_sem.at[t]
        )
        copy.start()
        results.append(copy)
    for copy in results:
        copy.wait()


def weight_sums(names, mine, other, shards, scale, after):
    n = len(shards)
    rows, cols = shards[0].shape
    width = mine.shape[1]
    tile = 768
    return pl.pallas_call(
        functools.partial(weight_kernel, names, tile, scale),
        out_shape=(
            jax.ShapeDtypeStruct((width, cols), jnp.float32),
            jax.ShapeDtypeStruct((8, 128), jnp.float32),
        ),
        in_specs=[VECTOR, VECTOR] + [IN_HBM] * n + [ANYWHERE] * len(after),
        out_specs=(IN_HBM, VECTOR),
        scratch_shapes=[
            pltpu.VMEM((width, n * rows), jnp.bfloat16),
            pltpu.VMEM((n * rows, cols), jnp.bfloat16),
            pltpu.VMEM((width, cols), jnp.float32),
            pltpu.SemaphoreType.DMA((n * (cols // tile),)),
            pltpu.SemaphoreType.DMA((cols // tile,)),
        ],
        compiler_params=params(),
        cost_estimate=NO_COST,
        name="weight_sums",
    )(mine, other, *shards, *after)


def body(grad_out, inputs, weight):
    rows = grad_out.shape[0]
    h = {"g": grad_out}

    first_early = (("d2", "u2"), ("u1", "ux1"))
    mixed = (("dx2", "g", "gx"), ("d3", "d1", "u3"))
    last_early = (("ux2",), ("dx3",))
    last = (("u4", "dx4"), ("dx1", "ux3"))

    def partials(groups, *after):
        return partial_sums(weight, [[h[s] for s in group] for group in groups], after)

    def slots(groups, *chosen):
        return [(k, (groups[0][k], groups[1][k])) for k in chosen]

    def over_y(parts):
        return [parts[0], in_y(parts[1], 1), in_y(parts[3], -1)]

    def phase(names, sends, *after, tokens=0):
        s = [h[name] for name in sends]
        moved = [up(s[0]), down(s[1])] + [across(v) for v in s[2:]]
        got = tie(moved + [h[n] for n in names[len(s) :]], after, tokens)
        h.update(zip(names, got))
        return got[len(names) :]

    mine = touch(inputs.T[None])
    pair = in_xh(mine)
    phase(("u1", "d1", "gx"), ("g", "g", "g"), pair)
    pair = stack(mine, pair, [h["u1"]])
    quad = in_y_pair(pair)
    phase(("u2", "d2", "ux1"), ("u1", "d1", "u1"), pair)
    quad = stack(pair, quad, [h["u2"]])
    column = in_y(quad, 2)
    keep_a, send_a = partials(first_early)
    got_a = in_core(send_a)
    phase(("u3", "d3", "dx2", "u2"), ("u2", "d2", "d2"), quad, keep_a)
    column = stack(quad, column, [h["u3"]])
    other = in_core(column)
    keep_b, send_b = partials(mixed)
    got_b = in_core(send_b)
    (token,) = phase(
        ("u4", "dx3", "ux2"), ("u3", "dx2", "u2"), column, got_a, keep_b, tokens=1
    )
    keep_c, send_c = partials(last_early, in_core(token))
    got_c = in_core(send_c)
    early = place(
        [
            (keep_a, got_a, slots(first_early, 0, 1)),
            (keep_b, got_b, slots(mixed, 0)),
            (keep_c, got_c, slots(last_early, 0)),
        ],
        [],
    )
    phase(("ux3", "dx4", "dx1"), ("ux2", "dx3", "d1"), other, *early)
    two_on = early[2]
    early = over_y(early)
    keep_d, send_d = partials(last)
    got_d = in_core(send_d)
    two_on, *late = place(
        [(keep_b, got_b, slots(mixed, 1, 2)), (keep_d, got_d, slots(last, 0, 1))],
        [two_on],
    )

    order = [s for groups in (first_early, mixed, last_early, last) for group in groups for s in group]
    grad_weight, token = weight_sums(
        order,
        column,
        other,
        [h[s] for s in order],
        1.0 / (Y * XH * C * rows),
        late,
    )

    early.append(in_y(two_on, 2))
    late = over_y(late) + [in_y(late[2], 2)]
    keep, send = merge(late, early, [token])
    grad_in = (keep + in_xh(send)).astype(jnp.bfloat16)
    return grad_in.T, grad_weight


def solution(mesh):
    return jax.shard_map(
        body,
        mesh=mesh,
        in_specs=(P("gx", "gy"), P("gy", "gx"), P("gx", "gy")),
        out_specs=(P("gy", "gx"), P("gx", "gy")),
        check_vma=False,
    )
```

```python
import functools

import jax
import jax.numpy as jnp
from jax import lax
from jax.experimental import pallas as pl
from jax.experimental.pallas import tpu as pltpu
from jax.sharding import PartitionSpec as P

XL, Z = 2, 8
Y, XH, C = 4, 2, 2
VMEM_LIMIT = 127 << 19
NO_COST = pl.CostEstimate(flops=1, bytes_accessed=1, transcendentals=0)


def gx_pairs(dxl, dz):
    return [
        (xl * Z + z, (xl + dxl) % XL * Z + (z + dz) % Z)
        for xl in range(XL)
        for z in range(Z)
    ]


def gy_pairs(dy, dxh, dc):
    return [
        (
            (y * XH + xh) * C + c,
            ((y + dy) % Y * XH + (xh + dxh) % XH) * C + (c + dc) % C,
        )
        for y in range(Y)
        for xh in range(XH)
        for c in range(C)
    ]


def up(t):
    return lax.ppermute(t, "gx", gx_pairs(0, 1))


def down(t):
    return lax.ppermute(t, "gx", gx_pairs(0, -1))


def across(t):
    return lax.ppermute(t, "gx", gx_pairs(1, 0))


def in_y_pair(t):
    pairs = [
        ((y * XH + xh) * C + c, ((y ^ 1) * XH + xh) * C + c)
        for y in range(Y)
        for xh in range(XH)
        for c in range(C)
    ]
    return lax.ppermute(t, "gy", pairs)


def in_y(t, dy):
    return lax.ppermute(t, "gy", gy_pairs(dy, 0, 0))


def in_xh(t):
    return lax.ppermute(t, "gy", gy_pairs(0, 1, 0))


def in_core(t):
    return lax.ppermute(t, "gy", gy_pairs(0, 0, 1))


AT = {"g": (0, 0), "gx": (1, 0)}
for _k in range(1, 5):
    AT[f"u{_k}"], AT[f"ux{_k}"] = (0, -_k), (1, -_k)
    AT[f"d{_k}"], AT[f"dx{_k}"] = (0, _k), (1, _k)


def position():
    ix, iy = lax.axis_index("gx"), lax.axis_index("gy")
    return ix >> 3, ix & 7, iy >> 2, (iy >> 1) & 1, iy & 1


def where(here, name):
    side, dz = AT[name]
    at = (here[1] + dz + Z) & 7
    return (here[0] ^ side) * 2 + (at >> 2), (at >> 1) & 1, at & 1


def keeps_even(here):
    return (here[1] & 1) == here[4]


def way(here, name):
    return (where(here, name)[0] - here[2]) & 3


def of_inputs(here, name):
    y, xh, c = where(here, name)
    dy = y ^ here[2]
    return (c ^ here[4]) * 8 + (dy >> 1) * 4 + (dy & 1) * 2 + (xh ^ here[3])


def ends_late(here):
    _, z, _, xh, c = here
    return ((z + ((z & 1) ^ c)) >> 1) & 1 == xh


IN_HBM = pl.BlockSpec(memory_space=pltpu.HBM)
ANYWHERE = pl.BlockSpec(memory_space=pl.ANY)
VECTOR = pl.BlockSpec(memory_space=pltpu.VMEM)


def params():
    return pltpu.CompilerParams(vmem_limit_bytes=VMEM_LIMIT)


def tie_kernel(n, *refs):
    for token_ref in refs[n:]:
        token_ref[...] = jnp.zeros_like(token_ref)


def tie(values, after, tokens):
    n = len(values)
    return pl.pallas_call(
        functools.partial(tie_kernel, 2 * n + len(after)),
        out_shape=[jax.ShapeDtypeStruct(v.shape, v.dtype) for v in values]
        + [jax.ShapeDtypeStruct((8, 128), jnp.float32)] * tokens,
        in_specs=[IN_HBM] * n + [ANYWHERE] * len(after),
        out_specs=[IN_HBM] * n + [VECTOR] * tokens,
        input_output_aliases={k: k for k in range(n)},
        compiler_params=params(),
        cost_estimate=NO_COST,
        name="tie",
    )(*values, *after)


def touch_kernel(a_ref, out_ref):
    out_ref[...] = a_ref[...]


def touch(a):
    return pl.pallas_call(
        touch_kernel,
        out_shape=jax.ShapeDtypeStruct(a.shape, a.dtype),
        in_specs=[VECTOR],
        out_specs=VECTOR,
        compiler_params=params(),
        cost_estimate=NO_COST,
        name="touch",
    )(a)


def stack_kernel(a_ref, b_ref, *refs):
    n = a_ref.shape[0]
    refs[-1][:n] = a_ref[...]
    refs[-1][n:] = b_ref[...]


def stack(a, b, after):
    return pl.pallas_call(
        stack_kernel,
        out_shape=jax.ShapeDtypeStruct((2 * a.shape[0],) + a.shape[1:], a.dtype),
        in_specs=[VECTOR] * 2 + [ANYWHERE] * len(after),
        out_specs=VECTOR,
        compiler_params=params(),
        cost_estimate=NO_COST,
        name="stack",
    )(a, b, *after)


PARTS = 4


def load_weight(w_any, w_ref, sem, first):
    part = w_ref.shape[0] // PARTS
    copies = []
    for k in range(PARTS):
        rows = pl.ds(k * part, part)
        copy = pltpu.make_async_copy(
            w_any.at[rows, :], w_ref.at[rows, :], sem.at[first + k]
        )
        copy.start()
        copies.append(copy)
    return copies


def product(w_ref, g_ref):
    return lax.dot_general(
        w_ref[...],
        g_ref[...],
        (((1,), (1,)), ((), ())),
        preferred_element_type=jnp.float32,
    )


def partial_kernel(places, w_any, *refs):
    n = len(places)
    pieces = refs[:n]
    keep_ref, send_ref, w_ref, g_ref, sem = refs[-5:]
    rows = keep_ref.shape[2]
    copies = load_weight(w_any, w_ref, sem, n)
    for k in range(n):
        copy = pltpu.make_async_copy(
            pieces[k], g_ref.at[pl.ds(k * rows, rows), :], sem.at[k]
        )
        copy.start()
        copies.append(copy)
    even = keeps_even(position())
    for copy in copies:
        copy.wait()
    sums = product(w_ref, g_ref)
    for k in range(n):
        group, slot = places[k]
        value = sums[:, k * rows : (k + 1) * rows]

        @pl.when(even == (group == 0))
        def _(slot=slot, value=value):
            keep_ref[slot] = value

        @pl.when(even == (group == 1))
        def _(slot=slot, value=value):
            send_ref[slot] = value


def partial_sums(weight, groups, after):
    places = [(g, k) for g, shards in enumerate(groups) for k in range(len(shards))]
    shards = [s for group in groups for s in group]
    n, slots = len(shards), max(len(group) for group in groups)
    rows, cols = shards[0].shape
    width = weight.shape[0]
    out = jax.ShapeDtypeStruct((slots, width, rows), jnp.float32)
    return pl.pallas_call(
        functools.partial(partial_kernel, places),
        out_shape=(out, out),
        in_specs=[IN_HBM] * (1 + n) + [ANYWHERE] * len(after),
        out_specs=(VECTOR, VECTOR),
        scratch_shapes=[
            pltpu.VMEM((width, cols), jnp.bfloat16),
            pltpu.VMEM((n * rows, cols), jnp.bfloat16),
            pltpu.SemaphoreType.DMA((n + PARTS,)),
        ],
        compiler_params=params(),
        cost_estimate=NO_COST,
        name="partial_sums",
    )(weight, *shards, *after)


def place_kernel(groups, *refs):
    n = 2 * len(groups)
    pairs, outs = refs[:n], refs[-Y:]
    extra = refs[n : n + (len(refs) - n - Y) // 2]
    for k, extra_ref in enumerate(extra):
        refs[-Y - 1 - k][...] = extra_ref[...]
    here = position()
    even = keeps_even(here)
    for group, slots in enumerate(groups):
        keep_ref, got_ref = pairs[2 * group], pairs[2 * group + 1]
        for i, names in slots:
            to = [-1 if name is None else way(here, name) for name in names]
            to = jnp.where(even, to[0], to[1])
            for r, out_ref in enumerate(outs):

                @pl.when(to == r)
                def _(keep_ref=keep_ref, got_ref=got_ref, i=i, out_ref=out_ref):
                    out_ref[...] = keep_ref[i] + got_ref[i]


def place(groups, extra):
    arrays = [a for kept, got, _ in groups for a in (kept, got)]
    out = jax.ShapeDtypeStruct(arrays[0].shape[1:], jnp.float32)
    return pl.pallas_call(
        functools.partial(place_kernel, [slots for _, _, slots in groups]),
        out_shape=[out] * (len(extra) + Y),
        in_specs=[VECTOR] * (len(arrays) + len(extra)),
        out_specs=[VECTOR] * (len(extra) + Y),
        compiler_params=params(),
        cost_estimate=NO_COST,
        name="place",
    )(*arrays, *extra)


def total_kernel(*refs):
    a, b, c, d = refs[:Y]
    refs[-1][...] = (a[...] + b[...]) + (c[...] + d[...])


def total(parts, after):
    return pl.pallas_call(
        total_kernel,
        out_shape=jax.ShapeDtypeStruct(parts[0].shape, jnp.float32),
        in_specs=[VECTOR] * Y + [ANYWHERE] * len(after),
        out_specs=VECTOR,
        compiler_params=params(),
        cost_estimate=NO_COST,
        name="total",
    )(*parts, *after)


def merge_kernel(*refs):
    late, early_ref, (keep_ref, send_ref) = refs[:Y], refs[Y], refs[-2:]
    a = (late[0][...] + late[1][...]) + (late[2][...] + late[3][...])
    b = early_ref[...]
    here = ends_late(position())
    keep_ref[...] = jnp.where(here, a, b)
    send_ref[...] = jnp.where(here, b, a)


def merge(late, early):
    out = jax.ShapeDtypeStruct(late[0].shape, jnp.float32)
    return pl.pallas_call(
        merge_kernel,
        out_shape=(out, out),
        in_specs=[VECTOR] * (Y + 1),
        out_specs=(VECTOR, VECTOR),
        compiler_params=params(),
        cost_estimate=NO_COST,
        name="merge",
    )(*late, early)


def weight_kernel(names, tile, scale, mine_ref, other_ref, *refs):
    n = len(names)
    pieces, (out_ref, token_ref) = refs[:n], refs[-7:-5]
    x_ref, g_ref, o_ref, in_sem, out_sem = refs[-5:]
    count, _, rows = mine_ref.shape
    tiles = g_ref.shape[1] // tile
    copies = []
    for t in range(tiles):
        columns = pl.ds(t * tile, tile)
        for k in range(n):
            copy = pltpu.make_async_copy(
                pieces[k].at[:, columns],
                g_ref.at[pl.ds(k * rows, rows), columns],
                in_sem.at[t * n + k],
            )
            copy.start()
            copies.append(copy)
    token_ref[...] = jnp.zeros_like(token_ref)
    here = position()
    for k, name in enumerate(names):
        at = of_inputs(here, name)
        target = slice(k * rows, (k + 1) * rows)

        @pl.when(at < count)
        def _(at=at, target=target):
            x_ref[:, target] = mine_ref[jnp.minimum(at, count - 1)]

        @pl.when(at >= count)
        def _(at=at, target=target):
            x_ref[:, target] = other_ref[jnp.maximum(at - count, 0)]

    results = []
    for t in range(tiles):
        columns = slice(t * tile, (t + 1) * tile)
        for copy in copies[t * n : (t + 1) * n]:
            copy.wait()
        sums = jnp.dot(
            x_ref[...], g_ref[:, columns], preferred_element_type=jnp.float32
        )
        o_ref[:, columns] = sums * scale
        copy = pltpu.make_async_copy(
            o_ref.at[:, columns], out_ref.at[:, columns], out_sem.at[t]
        )
        copy.start()
        results.append(copy)
    for copy in results:
        copy.wait()


def weight_sums(names, mine, other, shards, scale, after):
    n = len(shards)
    rows, cols = shards[0].shape
    width = mine.shape[1]
    tile = 768
    return pl.pallas_call(
        functools.partial(weight_kernel, names, tile, scale),
        out_shape=(
            jax.ShapeDtypeStruct((width, cols), jnp.float32),
            jax.ShapeDtypeStruct((8, 128), jnp.float32),
        ),
        in_specs=[VECTOR, VECTOR] + [IN_HBM] * n + [ANYWHERE] * len(after),
        out_specs=(IN_HBM, VECTOR),
        scratch_shapes=[
            pltpu.VMEM((width, n * rows), jnp.bfloat16),
            pltpu.VMEM((n * rows, cols), jnp.bfloat16),
            pltpu.VMEM((width, cols), jnp.float32),
            pltpu.SemaphoreType.DMA((n * (cols // tile),)),
            pltpu.SemaphoreType.DMA((cols // tile,)),
        ],
        compiler_params=params(),
        cost_estimate=NO_COST,
        name="weight_sums",
    )(mine, other, *shards, *after)


def body(grad_out, inputs, weight):
    rows = grad_out.shape[0]
    h = {"g": grad_out}

    first_early = (("d2", "u2"), ("u1", "ux1"))
    mixed = (("dx2", "g", "gx"), ("d3", "d1", "u3"))
    last_early = (("ux2",), ("dx3",))
    last = (("u4", "dx4"), ("dx1", "ux3"))

    def partials(groups, *after):
        return partial_sums(weight, [[h[s] for s in group] for group in groups], after)

    def slots(groups, *chosen):
        return [(k, (groups[0][k], groups[1][k])) for k in chosen]

    def over_y(parts):
        return [parts[0], in_y(parts[1], 1), in_y(parts[3], -1)]

    def phase(names, sends, *after, tokens=0):
        s = [h[name] for name in sends]
        moved = [up(s[0]), down(s[1])] + [across(v) for v in s[2:]]
        got = tie(moved + [h[n] for n in names[len(s) :]], after, tokens)
        h.update(zip(names, got))
        return got[len(names) :]

    mine = touch(inputs.T[None])
    pair = in_xh(mine)
    phase(("u1", "d1", "gx"), ("g", "g", "g"), pair)
    pair = stack(mine, pair, [h["u1"]])
    quad = in_y_pair(pair)
    phase(("u2", "d2", "ux1"), ("u1", "d1", "u1"), pair)
    quad = stack(pair, quad, [h["u2"]])
    column = in_y(quad, 2)
    keep_a, send_a = partials(first_early)
    got_a = in_core(send_a)
    phase(("u3", "d3", "dx2", "u2"), ("u2", "d2", "d2"), quad, keep_a)
    column = stack(quad, column, [h["u3"]])
    other = in_core(column)
    keep_b, send_b = partials(mixed)
    got_b = in_core(send_b)
    (token,) = phase(
        ("u4", "dx3", "ux2"), ("u3", "dx2", "u2"), column, got_a, keep_b, tokens=1
    )
    keep_c, send_c = partials(last_early, in_core(token))
    got_c = in_core(send_c)
    early = place(
        [
            (keep_a, got_a, slots(first_early, 0, 1)),
            (keep_b, got_b, slots(mixed, 0)),
            (keep_c, got_c, slots(last_early, 0)),
        ],
        [],
    )
    phase(("ux3", "dx4", "dx1"), ("ux2", "dx3", "d1"), other, *early)
    two_on = early[2]
    early = over_y(early)
    keep_d, send_d = partials(last)
    got_d = in_core(send_d)
    two_on, *late = place(
        [(keep_b, got_b, slots(mixed, 1, 2)), (keep_d, got_d, slots(last, 0, 1))],
        [two_on],
    )

    order = [s for groups in (first_early, mixed, last_early, last) for group in groups for s in group]
    grad_weight, token = weight_sums(
        order,
        column,
        other,
        [h[s] for s in order],
        1.0 / (Y * XH * C * rows),
        late,
    )

    early.append(in_y(two_on, 2))
    late = over_y(late) + [in_y(late[2], 2)]
    keep, send = merge(late, total(early, [token]))
    grad_in = (keep + in_xh(send)).astype(jnp.bfloat16)
    return grad_in.T, grad_weight


def solution(mesh):
    return jax.shard_map(
        body,
        mesh=mesh,
        in_specs=(P("gx", "gy"), P("gy", "gx"), P("gx", "gy")),
        out_specs=(P("gy", "gx"), P("gx", "gy")),
        check_vma=False,
    )
```
